512 devices in a mesh: sector: 8 (over z_hi, x), term: 64 (over y, z_lo, core).
Axes of the slice: x: 4, y: 8, z: 8 (z_hi: 2, z_lo: 4; z = z_hi * 4 + z_lo), core: 2. Of those that a mesh axis runs over, the one named last changes fastest.
Arguments:
- trial: bfloat16 [4096, 1024], P(('sector', 'term')), may hold values from -6 to 6
- block_rows: int32 [16], P('sector'), may hold values from 64 to 256, as said below
- right_ops: bfloat16 [512, 1024, 1024], P(('sector', 'term')), may hold values from -0.1875 to 0.1875
- left_ops: bfloat16 [512, 8, 256, 256], P(('sector', 'term')), may hold values from -0.046875 to 0.046875
- ent_source: int32 [512, 8], P(('sector', 'term')), may hold values from 0 to 3
- ent_target: int32 [512, 8], P(('sector', 'term')), may hold values from 0 to 1
- ent_count: int32 [512], P(('sector', 'term')), may hold values from 1 to 8, as said below
Outputs:
- sigma: bfloat16 [4096, 1024], P(('sector', 'term'))
The draws below stay inside these ranges and needn't reach their ends.
Inputs may be any that keep to these rules, and one draw needn't show every extreme that they name: `block_rows`: some block has exactly 256 rows in every draw. Only entries k < ent_count[t] of term t are live; some term has 8 live entries in every draw.
All inputs are finite; a program needn't handle non-finite values.
Results may differ from the reference program's by a relative error of at most 0.005.
Values may be sent and summed in bfloat16 or wider, within the bound.
A program may use at most 64 MiB of HBM per device.

```python
import jax
import jax.numpy as jnp
from jax import lax

M = 1024
BR = 256
SEC_GRP = 2
ENT = 8
SECTORS = 16
TERMS = 512
ROWS = 4096
N_TERM = 64


def draw_block_rows(key, part):
    key = jax.random.fold_in(key, 11)
    first_key, second_key = jax.random.split(key)
    values = jax.random.randint(first_key, (SECTORS,), BR // 4, BR + 1, dtype=jnp.int32)
    chosen = jax.random.randint(second_key, (), 0, SECTORS, dtype=jnp.int32)
    return jnp.where(jnp.arange(SECTORS, dtype=jnp.int32) == chosen, BR, values).astype(jnp.int32)


def draw_ent_count(key, part):
    key = jax.random.fold_in(key, 23)
    first_key, second_key, third_key = jax.random.split(key, 3)
    base_count = jax.random.randint(first_key, (TERMS,), 1, max(ENT // 4, 1) + 1, dtype=jnp.int32)
    heavy = jax.random.randint(second_key, (TERMS,), 0, 8, dtype=jnp.int32) == 0
    chosen = jax.random.randint(third_key, (), 0, TERMS, dtype=jnp.int32)
    values = jnp.where(heavy, ENT, base_count)
    return jnp.where(jnp.arange(TERMS, dtype=jnp.int32) == chosen, ENT, values).astype(jnp.int32)


def touch_ends(array, stream_key, least, top_value):
    longest = array.shape.index(max(array.shape))
    spots = []
    for shift in (0, 1):
        where = [jax.random.randint(jax.random.fold_in(stream_key, axis), (), 0, length) for axis, length in enumerate(array.shape)]
        where[longest] = (where[longest] + shift) % array.shape[longest]
        spots.append(tuple(where))
    return array.at[spots[0]].set(least).at[spots[1]].set(top_value)


def levels(rng, shape, cuts, smallest, top_value):
    def one(dim, shards_of):
        heights = jax.random.uniform(jax.random.fold_in(jax.random.fold_in(rng, 6), dim), (shards_of,), jnp.float32, smallest / len(cuts), top_value / len(cuts))
        return jnp.repeat(jnp.exp(heights), shape[dim] // shards_of).reshape((-1,) + (1,) * (len(shape) - dim - 1))

    factor_of = one(*cuts[0])
    for cut in cuts[1:]:
        factor_of = factor_of * one(*cut)
    return factor_of


def normal_values(stream_key, dims, spread, most, cuts=(), kind=jnp.bfloat16):
    values = jax.random.normal(stream_key, dims, jnp.float32) * spread
    if len(cuts) > 0:
        values = levels(stream_key, dims, cuts, -0.22, 0.18) * values
    return jnp.clip(values, min=-most, max=most).astype(kind)


def setup_inputs(seed: int = 0) -> dict:
    keys = jax.random.split(jax.random.key(seed), 8)
    trial = normal_values(keys[0], (ROWS, M), 1.0, 6.0, ((0, 512),))
    block_rows = draw_block_rows(jax.random.fold_in(keys[7], 71), 0)
    right_ops = normal_values(keys[2], (TERMS, M, M), M ** -0.5, 0.1875, ((0, 512),))
    left_ops = normal_values(keys[3], (TERMS, ENT, BR, BR), (BR * N_TERM) ** -0.5, 0.046875, ((0, 512),))
    ent_source = touch_ends(jax.random.randint(keys[4], (TERMS, ENT), 0, 2 * SEC_GRP), jax.random.fold_in(keys[4], 1), 0, (2 * SEC_GRP) - 1).astype(jnp.int32)
    ent_target = touch_ends(jax.random.randint(keys[5], (TERMS, ENT), 0, SEC_GRP), jax.random.fold_in(keys[5], 1), 0, SEC_GRP - 1).astype(jnp.int32)
    ent_count = draw_ent_count(jax.random.fold_in(keys[7], 71), 0)
    return dict(trial=trial, block_rows=block_rows, right_ops=right_ops, left_ops=left_ops, ent_source=ent_source, ent_target=ent_target, ent_count=ent_count)


def reference(trial, block_rows, right_ops, left_ops, ent_source, ent_target, ent_count):
    sectors = block_rows.shape[0]
    block_len = left_ops.shape[2]
    columns = trial.shape[1]
    keep_rows = jnp.arange(block_len, dtype=jnp.int32)[None, :] < block_rows[:, None]
    blocks = jnp.where(keep_rows[:, :, None], trial.reshape(sectors, block_len, columns), jnp.zeros((), trial.dtype))
    padded = jnp.concatenate([jnp.zeros((SEC_GRP, block_len, columns), trial.dtype), blocks], 0)

    def one_term(totals, term_id):
        group_id = term_id // N_TERM
        own_blocks = lax.dynamic_slice_in_dim(padded, (group_id + 1) * SEC_GRP, SEC_GRP, 0)
        prior_blocks = lax.dynamic_slice_in_dim(padded, group_id * SEC_GRP, SEC_GRP, 0)
        window = jnp.concatenate([own_blocks, prior_blocks], 0).reshape(2 * SEC_GRP * block_len, columns)
        operator = lax.dynamic_index_in_dim(right_ops, term_id, 0, keepdims=False)
        projected = jnp.dot(window, operator, preferred_element_type=jnp.float32).astype(jnp.bfloat16)
        projected = projected.reshape(2 * SEC_GRP, block_len, columns)
        lefts = lax.dynamic_index_in_dim(left_ops, term_id, 0, keepdims=False)
        sources = lax.dynamic_index_in_dim(ent_source, term_id, 0, keepdims=False)
        targets = lax.dynamic_index_in_dim(ent_target, term_id, 0, keepdims=False)
        live_count = lax.dynamic_index_in_dim(ent_count, term_id, 0, keepdims=False)

        def add_entry(slot, inner):
            one_block = lax.dynamic_index_in_dim(projected, sources[slot], 0, keepdims=False)
            left_op = lax.dynamic_index_in_dim(lefts, slot, 0, keepdims=False)
            product = jnp.dot(left_op, one_block, preferred_element_type=jnp.float32)
            weight = (slot < live_count).astype(inner.dtype)
            target_id = (group_id * SEC_GRP + targets[slot]).astype(jnp.int32)
            current = lax.dynamic_index_in_dim(inner, target_id, 0, keepdims=False)
            return lax.dynamic_update_index_in_dim(inner, current + weight * product.astype(inner.dtype), target_id, 0)

        return lax.fori_loop(0, ENT, add_entry, totals), None

    start = jnp.zeros((sectors, block_len, columns), jnp.float32)
    totals, unused = lax.scan(one_term, start, jnp.arange(sectors // SEC_GRP * N_TERM, dtype=jnp.int32))
    result = jnp.where(keep_rows[:, :, None], totals, jnp.zeros((), totals.dtype))
    return result.reshape(sectors * block_len, columns).astype(jnp.bfloat16)
```

```python
import functools

import jax
import jax.numpy as jnp
from jax import lax
from jax.experimental import pallas as pl
from jax.experimental.pallas import tpu as pltpu
from jax.sharding import PartitionSpec as P

MESH = pl.DeviceIdType.MESH
F32 = jnp.float32
BF16 = jnp.bfloat16


def kernel(
    sectors, ny, nz,
    trial_ref, rows_ref, right_ref, left_ref, source_ref, target_ref, count_ref,
    out_ref,
    units, window, lefts, weights, weights_sib, right_own, right_sib, projected, outgoing, incoming,
    load_sem, pair_send, pair_recv, next_send, next_recv, z_send, z_recv, y_send, y_recv,
    d_send, d_recv, r_send, r_recv,
):
    entries, block_len = lefts.shape[0], lefts.shape[1]
    columns = right_own.shape[0]
    half = columns // 2
    group_rows = 2 * block_len
    chips = ny * nz
    far = ny // 2
    s = lax.axis_index("sector")
    t = lax.axis_index("term")
    y, z, c = t // (2 * nz), lax.rem(t // 2, nz), lax.rem(t, 2)
    me = t // 2

    def device(sector, chip, core):
        return (sector, chip * 2 + core)

    sibling = device(s, me, 1 - c)
    following = device(lax.rem(s + 1, sectors), me, c)
    preceding = device(lax.rem(s + sectors - 1, sectors), me, c)

    load_left = pltpu.make_async_copy(left_ref.at[0], lefts, load_sem.at[0])
    load_right = pltpu.make_async_copy(right_ref.at[0], right_own, load_sem.at[1])
    load_left.start()
    load_right.start()

    barrier = pltpu.get_barrier_semaphore()

    def greet(j, carry):
        chip = lax.rem(me + j, chips)
        pl.semaphore_signal(barrier, inc=1, device_id=device(s, chip, c), device_id_type=MESH)
        return carry

    pl.semaphore_signal(barrier, inc=1, device_id=sibling, device_id_type=MESH)
    pl.semaphore_signal(barrier, inc=1, device_id=preceding, device_id_type=MESH)
    lax.fori_loop(1, chips, greet, 0)

    start_row = t * 8
    limit = rows_ref[start_row // block_len]
    inside = lax.rem(start_row, block_len) + lax.broadcasted_iota(jnp.int32, (8, columns), 0)
    live_rows = inside < limit
    own = jnp.where(live_rows, trial_ref[...].astype(F32), 0.0)
    own = jnp.concatenate([own[:, :half], own[:, half:]], axis=0)
    units[0, c, y, z] = own.astype(BF16)

    load_left.wait()
    count = count_ref[0]
    factors = []
    for k in range(entries):
        live = k < count
        src, dst = source_ref[0, k], target_ref[0, k]
        for b in range(2):
            for w in range(4):
                on = live & (dst == b) & (src == w)
                if w >= 2:
                    on = on & (s > 0)
                factors.append(jnp.where(on, 1.0, 0.0).astype(F32))

    def weigh(i, carry):
        row = pl.multiple_of(i * 32, 32)
        blocks = [lefts[k, pl.ds(row, 32), :].astype(F32) for k in range(entries)]
        at = pl.multiple_of(i * 16, 16)
        for b in range(2):
            for w in range(4):
                total = blocks[0] * factors[b * 4 + w]
                for k in range(1, entries):
                    total = total + blocks[k] * factors[k * 8 + b * 4 + w]
                total = total.reshape(2, 2, 8, block_len)
                for p in range(2):
                    piece = total[:, p].reshape(16, block_len).astype(BF16)
                    weights[p, pl.ds(b * (block_len // 2) + at, 16), w * block_len:(w + 1) * block_len] = piece
        return carry

    lax.fori_loop(0, block_len // 32, weigh, 0)

    pl.semaphore_wait(barrier, chips - 1 + 2)

    def remote(source, destination, send, recv, target):
        return pltpu.make_async_remote_copy(
            src_ref=source, dst_ref=destination, send_sem=send, recv_sem=recv,
            device_id=target, device_id_type=MESH,
        )

    sends = []

    def begin(copy):
        copy.start()
        sends.append(copy)
        return copy

    def z_copies(st):
        slot = units.at[st, c, y, z]
        return [
            remote(slot, slot, z_send.at[st, d - 1], z_recv.at[st, d - 1],
                   device(s, y * nz + lax.rem(z + d, nz), c))
            for d in range(1, nz)
        ]

    def slab(st, way, k):
        row = lax.rem(y - k + ny, ny) if way == 0 else lax.rem(y + k, ny)
        if k < far:
            return units.at[st, c, row]
        return units.at[st, c, row, pl.ds(way * (nz // 2), nz // 2)]

    def y_copy(st, way, k):
        row = lax.rem(y - (k - 1) + ny, ny) if way == 0 else lax.rem(y + (k - 1), ny)
        if k < far:
            slot = units.at[st, c, row]
        else:
            slot = units.at[st, c, row, pl.ds(way * (nz // 2), nz // 2)]
        to = lax.rem(y + 1, ny) if way == 0 else lax.rem(y + ny - 1, ny)
        return remote(slot, slot, y_send.at[st, way, k - 1], y_recv.at[st, way, k - 1],
                      device(s, to * nz + z, c))

    def d_copy(st, way, k):
        index = 0 if k == 0 else way * far + k
        slot = units.at[st, c, y] if k == 0 else slab(st, way, k)
        return remote(slot, slot, d_send.at[st, index], d_recv.at[st, index], sibling)

    z_all = [z_copies(st) for st in range(2)]
    for copy in z_all[0]:
        begin(copy)
    next_copy = begin(remote(units.at[0, c, y, z], units.at[1, c, y, z], next_send.at[0], next_recv.at[0], following))
    weights_copy = begin(remote(weights.at[1 - c], weights_sib, pair_send.at[0], pair_recv.at[0], sibling))
    right_copy = begin(remote(right_ref.at[0], right_sib, pair_send.at[1], pair_recv.at[1], sibling))

    steps = {}
    pairs = []

    def begin_y(st, way, k):
        steps[st, way, k] = begin(y_copy(st, way, k))

    def begin_d(st, way, k):
        pairs.append((st, begin(d_copy(st, way, k))))

    for st in range(2):
        if st == 1:
            next_copy.wait_recv()
            for copy in z_all[1]:
                begin(copy)
        for copy in z_all[st]:
            copy.wait_recv()
        begin_y(st, 0, 1)
        begin_y(st, 1, 1)
        begin_d(st, 0, 0)
    for k in range(1, far + 1):
        for st in range(2):
            for way in range(2):
                steps[st, way, k].wait_recv()
                if k < far:
                    begin_y(st, way, k + 1)
                begin_d(st, way, k)

    def lay(st):
        def one(row, carry):
            pieces = [units[st, p, row].astype(F32).reshape(nz, 2, 8, half) for p in range(2)]
            at = pl.multiple_of(st * group_rows + row * (nz * 16), 16)
            for h in range(2):
                both = jnp.concatenate([pieces[0][:, h:h + 1], pieces[1][:, h:h + 1]], axis=1)
                window[pl.ds(at, nz * 16), h * half:(h + 1) * half] = both.reshape(nz * 16, half).astype(BF16)
            return carry

        lax.fori_loop(0, ny, one, 0)

    for st in range(2):
        for which, copy in pairs:
            if which == st:
                copy.wait_recv()
        lay(st)

    weights_copy.wait_recv()
    right_copy.wait_recv()
    load_right.wait()
    tile = min(256, half)
    for n in range(columns // tile):
        part = window[:, n * tile:(n + 1) * tile]
        projected[:, n * tile:(n + 1) * tile] = jnp.dot(
            weights[c], part, preferred_element_type=F32).astype(BF16)
        projected[:, columns + n * tile:columns + (n + 1) * tile] = jnp.dot(
            weights_sib[...], part, preferred_element_type=F32).astype(BF16)

    for n in range(half // tile):
        both = []
        for h in range(2):
            at = h * half + n * tile
            value = jnp.dot(projected[:, :columns], right_own[:, at:at + tile], preferred_element_type=F32)
            value = value + jnp.dot(projected[:, columns:], right_sib[:, at:at + tile], preferred_element_type=F32)
            both.append(value.reshape(chips, 8, tile))
        outgoing[:, :, n * tile:(n + 1) * tile] = jnp.concatenate(both, axis=1).astype(BF16)

    def scatter_copy(chip):
        return remote(outgoing.at[chip], incoming.at[me], r_send.at[chip], r_recv.at[me], device(s, chip, c))

    def scatter(j, carry):
        scatter_copy(lax.rem(me + j, chips)).start()
        return carry

    order = [far]
    for k in range(far - 1, -1, -1):
        order += [k, ny - k] if k else [0]
    for dy in order:
        row = lax.rem(y + dy, ny)
        for dz in range(nz - 1, -1, -1):
            if dy or dz:
                scatter_copy(row * nz + lax.rem(z + dz, nz)).start()
    incoming[me] = outgoing[me]

    def gathered(j, carry):
        chip = lax.rem(me + j, chips)
        remote(outgoing.at[chip], incoming.at[chip], r_send.at[chip], r_recv.at[chip], device(s, chip, c)).wait_recv()
        return carry

    lax.fori_loop(1, chips, gathered, 0)
    total = incoming[0].astype(F32)
    for chip in range(1, chips):
        total = total + incoming[chip].astype(F32)
    result = jnp.concatenate([total[0:8], total[8:16]], axis=1)
    out_ref[...] = jnp.where(live_rows, result, 0.0).astype(BF16)

    for copy in sends:
        copy.wait_send()

    def sent(j, carry):
        chip = lax.rem(me + j, chips)
        remote(outgoing.at[chip], incoming.at[chip], r_send.at[chip], r_recv.at[chip], device(s, chip, c)).wait_send()
        return carry

    lax.fori_loop(1, chips, sent, 0)


def local(sectors, ny, nz, trial, block_rows, right_ops, left_ops, ent_source, ent_target, ent_count):
    entries, block_len = left_ops.shape[1:3]
    columns = trial.shape[1]
    chips = ny * nz
    far = ny // 2
    dma = pltpu.SemaphoreType.DMA
    vmem = pl.BlockSpec(memory_space=pltpu.VMEM)
    smem = pl.BlockSpec(memory_space=pltpu.SMEM)
    hbm = pl.BlockSpec(memory_space=pl.ANY)
    return pl.pallas_call(
        functools.partial(kernel, sectors, ny, nz),
        out_shape=jax.ShapeDtypeStruct(trial.shape, trial.dtype),
        in_specs=[vmem, smem, hbm, hbm, smem, smem, smem],
        out_specs=vmem,
        scratch_shapes=[
            pltpu.VMEM((2, 2, ny, nz, 16, columns // 2), BF16),
            pltpu.VMEM((4 * block_len, columns), BF16),
            pltpu.VMEM((entries, block_len, block_len), BF16),
            pltpu.VMEM((2, block_len, 4 * block_len), BF16),
            pltpu.VMEM((block_len, 4 * block_len), BF16),
            pltpu.VMEM((columns, columns), BF16),
            pltpu.VMEM((columns, columns), BF16),
            pltpu.VMEM((block_len, 2 * columns), BF16),
            pltpu.VMEM((chips, 16, columns // 2), BF16),
            pltpu.VMEM((chips, 16, columns // 2), BF16),
            dma((2,)), dma((2,)), dma((2,)), dma((1,)), dma((1,)),
            dma((2, nz - 1)), dma((2, nz - 1)),
            dma((2, 2, far)), dma((2, 2, far)),
            dma((2, 2 * far + 1)), dma((2, 2 * far + 1)),
            dma((chips,)), dma((chips,)),
        ],
        compiler_params=pltpu.CompilerParams(
            collective_id=0, has_side_effects=True, vmem_limit_bytes=48 * 1024 * 1024,
        ),
        name="sigma",
    )(trial, block_rows, right_ops, left_ops, ent_source, ent_target, ent_count)


def solution(mesh):
    nz = 4
    sectors = mesh.shape["sector"]
    ny = mesh.shape["term"] // (2 * nz)
    placed = (
        P(("sector", "term"), None),
        P("sector"),
        P(("sector", "term"), None, None),
        P(("sector", "term"), None, None, None),
        P(("sector", "term"), None),
        P(("sector", "term"), None),
        P(("sector", "term")),
    )
    return jax.shard_map(
        functools.partial(local, sectors, ny, nz), mesh=mesh, in_specs=placed,
        out_specs=P(("sector", "term"), None), check_vma=False,
    )
```

```python
import functools

import jax
import jax.numpy as jnp
from jax import lax
from jax.experimental import pallas as pl
from jax.experimental.pallas import tpu as pltpu
from jax.sharding import PartitionSpec as P

MESH = pl.DeviceIdType.MESH
F32 = jnp.float32
BF16 = jnp.bfloat16


def kernel(
    sectors, ny, nz,
    trial_in, rows_in, right_ref, left_ref, source_in, target_in, count_in,
    out_ref,
    trial_ref, rows_ref, source_ref, target_ref, count_ref,
    units, window, lefts, weights, weights_sib, right_own, right_sib, projected, outgoing, incoming,
    passed, passed_half,
    load_sem, pair_send, pair_recv, next_send, next_recv, z_send, z_recv, y_send, y_recv,
    d_send, d_recv, m_send, m_recv, r_send, r_recv,
):
    entries, block_len = lefts.shape[0], lefts.shape[1]
    columns = right_own.shape[0]
    half = columns // 2
    group_rows = 2 * block_len
    chips = ny * nz
    far = ny // 2
    s = lax.axis_index("sector")
    t = lax.axis_index("term")
    y, z, c = t // (2 * nz), lax.rem(t // 2, nz), lax.rem(t, 2)
    me = t // 2

    def device(sector, chip, core):
        return (sector, chip * 2 + core)

    sibling = device(s, me, 1 - c)
    following = lax.rem(s + 1, sectors)
    preceding = lax.rem(s + sectors - 1, sectors)

    def near(dy, dz):
        return lax.rem(y + dy + ny, ny) * nz + lax.rem(z + dz, nz)


    loads = [
        pltpu.make_async_copy(source, destination, load_sem.at[i])
        for i, (source, destination) in enumerate([
            (trial_in, trial_ref), (rows_in, rows_ref), (source_in, source_ref), (target_in, target_ref),
            (count_in, count_ref), (left_ref.at[0], lefts), (right_ref.at[0], right_own),
        ])
    ]
    for load in loads:
        load.start()

    barrier = pltpu.get_barrier_semaphore()

    def greet(target):
        pl.semaphore_signal(barrier, inc=1, device_id=target, device_id_type=MESH)

    greet(sibling)
    for dz in range(nz):
        greet(device(preceding, near(0, dz), c))
    for dy in range(-2, 3):
        for dz in range(nz):
            if dy or dz:
                greet(device(s, near(dy, dz), c))

    loads[0].wait()
    loads[1].wait()
    start_row = t * 8
    limit = rows_ref[start_row // block_len]
    inside = lax.rem(start_row, block_len) + lax.broadcasted_iota(jnp.int32, (8, columns), 0)
    live_rows = inside < limit
    own = jnp.where(live_rows, trial_ref[...].astype(F32), 0.0)
    own = jnp.concatenate([own[:, :half], own[:, half:]], axis=0)
    units[0, c, y, z] = own.astype(BF16)

    pl.semaphore_wait(barrier, 1 + nz + 5 * nz - 1)

    def remote(source, destination, send, recv, target):
        return pltpu.make_async_remote_copy(
            src_ref=source, dst_ref=destination, send_sem=send, recv_sem=recv,
            device_id=target, device_id_type=MESH,
        )

    sends = []

    def begin(copy):
        copy.start()
        sends.append(copy)
        return copy

    def z_copies():
        slot = units.at[0, c, y, z]
        return [
            remote(slot, slot, z_send.at[d - 1], z_recv.at[d - 1], device(s, near(0, d), c))
            for d in range(1, nz)
        ]

    def slab(st, way, k):
        row = lax.rem(y - k + ny, ny) if way == 0 else lax.rem(y + k, ny)
        if k < far:
            return units.at[st, c, row]
        return units.at[st, c, row, pl.ds(way * (nz // 2), nz // 2)]

    def y_copy(st, way, k):
        row = lax.rem(y - (k - 1) + ny, ny) if way == 0 else lax.rem(y + (k - 1), ny)
        if k < far:
            slot = units.at[st, c, row]
        else:
            slot = units.at[st, c, row, pl.ds(way * (nz // 2), nz // 2)]
        to = lax.rem(y + 1, ny) if way == 0 else lax.rem(y + ny - 1, ny)
        return remote(slot, slot, y_send.at[st, way, k - 1], y_recv.at[st, way, k - 1],
                      device(s, to * nz + z, c))

    def d_copy(st, way, k):
        index = 0 if k == 0 else way * far + k
        slot = units.at[st, c, y] if k == 0 else slab(st, way, k)
        return remote(slot, slot, d_send.at[st, index], d_recv.at[st, index], sibling)

    z_all = [begin(copy) for copy in z_copies()]
    next_all = [
        begin(remote(units.at[0, c, y, z], units.at[1, c, y, z], next_send.at[d], next_recv.at[d],
                     device(following, near(0, d), c)))
        for d in range(nz)
    ]
    right_copy = begin(remote(right_ref.at[0], right_sib, pair_send.at[1], pair_recv.at[1], sibling))

    for load in loads[2:6]:
        load.wait()
    count = count_ref[0, 0]
    factors = []
    for k in range(entries):
        live = k < count
        src, dst = source_ref[0, k], target_ref[0, k]
        for b in range(2):
            for w in range(4):
                on = live & (dst == b) & (src == w)
                if w >= 2:
                    on = on & (s > 0)
                factors.append(jnp.where(on, 1.0, 0.0).astype(F32))

    def weigh(i, carry):
        row = pl.multiple_of(i * 32, 32)
        blocks = [lefts[k, pl.ds(row, 32), :].astype(F32) for k in range(entries)]
        at = pl.multiple_of(i * 16, 16)
        for b in range(2):
            for w in range(4):
                total = blocks[0] * factors[b * 4 + w]
                for k in range(1, entries):
                    total = total + blocks[k] * factors[k * 8 + b * 4 + w]
                total = total.reshape(2, 2, 8, block_len)
                for p in range(2):
                    piece = total[:, p].reshape(16, block_len).astype(BF16)
                    weights[p, pl.ds(b * (block_len // 2) + at, 16), w * block_len:(w + 1) * block_len] = piece
        return carry

    lax.fori_loop(0, block_len // 32, weigh, 0)

    weights_copy = begin(remote(weights.at[1 - c], weights_sib, pair_send.at[0], pair_recv.at[0], sibling))

    steps = {}
    pairs = []

    def begin_y(st, way, k):
        steps[st, way, k] = begin(y_copy(st, way, k))

    def begin_d(st, way, k):
        pairs.append((st, begin(d_copy(st, way, k))))

    for st in range(2):
        for copy in (next_all if st else z_all):
            copy.wait_recv()
        begin_y(st, 0, 1)
        begin_y(st, 1, 1)
        begin_d(st, 0, 0)
    for k in range(1, far + 1):
        for st in range(2):
            for way in range(2):
                steps[st, way, k].wait_recv()
                if k < far:
                    begin_y(st, way, k + 1)
                begin_d(st, way, k)

    def lay(st):
        def one(row, carry):
            pieces = [units[st, p, row].astype(F32).reshape(nz, 2, 8, half) for p in range(2)]
            at = pl.multiple_of(st * group_rows + row * (nz * 16), 16)
            for h in range(2):
                both = jnp.concatenate([pieces[0][:, h:h + 1], pieces[1][:, h:h + 1]], axis=1)
                window[pl.ds(at, nz * 16), h * half:(h + 1) * half] = both.reshape(nz * 16, half).astype(BF16)
            return carry

        lax.fori_loop(0, ny, one, 0)

    for st in range(2):
        for which, copy in pairs:
            if which == st:
                copy.wait_recv()
        lay(st)

    weights_copy.wait_recv()
    right_copy.wait_recv()
    loads[6].wait()
    tile = min(256, half)
    for n in range(columns // tile):
        part = window[:, n * tile:(n + 1) * tile]
        projected[:, n * tile:(n + 1) * tile] = jnp.dot(
            weights[c], part, preferred_element_type=F32).astype(BF16)
        projected[:, columns + n * tile:columns + (n + 1) * tile] = jnp.dot(
            weights_sib[...], part, preferred_element_type=F32).astype(BF16)

    for n in range(half // tile):
        both = []
        for h in range(2):
            at = h * half + n * tile
            value = jnp.dot(projected[:, :columns], right_own[:, at:at + tile], preferred_element_type=F32)
            value = value + jnp.dot(projected[:, columns:], right_sib[:, at:at + tile], preferred_element_type=F32)
            both.append(value.reshape(chips, 8, tile))
        outgoing[:, :, n * tile:(n + 1) * tile] = jnp.concatenate(both, axis=1).astype(BF16)

    def row_at(dy):
        return lax.rem(y + dy + ny, ny) * nz

    merged = []
    for way, sign in ((0, 1), (1, -1)):
        merged.append((
            begin(remote(outgoing.at[pl.ds(row_at(3 * sign), nz)], passed.at[way],
                         m_send.at[way, 0], m_recv.at[way, 0], device(s, near(sign, 0), c))),
            begin(remote(outgoing.at[pl.ds(row_at(4) + way * (nz // 2), nz // 2)], passed_half.at[way],
                         m_send.at[way, 1], m_recv.at[way, 1], device(s, near(2 * sign, 0), c))),
        ))

    finals = []

    def deliver(dy, dz):
        chip = near(dy, dz)
        finals.append(begin(remote(
            outgoing.at[chip], incoming.at[(2 + dy) * nz + z],
            r_send.at[(2 + dy) * nz + dz], r_recv.at[(2 + dy) * nz + dz], device(s, chip, c))))

    for dy in (1, -1, 0):
        for dz in range(nz - 1, -1, -1):
            if dy or dz:
                deliver(dy, dz)
    incoming[2 * nz + z] = outgoing[me]
    for way, sign in ((0, 1), (1, -1)):
        whole, part = merged[way]
        whole.wait_recv()
        part.wait_recv()
        for i in range(nz):
            at = row_at(2 * sign) + i
            value = outgoing[at].astype(F32) + passed[way, i].astype(F32)
            if i // (nz // 2) == way:
                value = value + passed_half[way, i % (nz // 2)].astype(F32)
            outgoing[at] = value.astype(BF16)
        for dz in range(nz - 1, -1, -1):
            deliver(2 * sign, dz)

    for copy in finals:
        copy.wait_recv()
    total = incoming[0].astype(F32)
    for i in range(1, 5 * nz):
        total = total + incoming[i].astype(F32)
    result = jnp.concatenate([total[0:8], total[8:16]], axis=1)
    out_ref[...] = jnp.where(live_rows, result, 0.0).astype(BF16)

    for copy in sends:
        copy.wait_send()


def local(sectors, ny, nz, trial, block_rows, right_ops, left_ops, ent_source, ent_target, ent_count):
    entries, block_len = left_ops.shape[1:3]
    columns = trial.shape[1]
    chips = ny * nz
    far = ny // 2
    dma = pltpu.SemaphoreType.DMA
    vmem = pl.BlockSpec(memory_space=pltpu.VMEM)
    hbm = pl.BlockSpec(memory_space=pl.ANY)
    return pl.pallas_call(
        functools.partial(kernel, sectors, ny, nz),
        out_shape=jax.ShapeDtypeStruct(trial.shape, trial.dtype),
        in_specs=[hbm] * 7,
        out_specs=vmem,
        scratch_shapes=[
            pltpu.VMEM(trial.shape, trial.dtype),
            pltpu.SMEM(block_rows.shape, jnp.int32),
            pltpu.SMEM(ent_source.shape, jnp.int32),
            pltpu.SMEM(ent_target.shape, jnp.int32),
            pltpu.SMEM((1, 1), jnp.int32),
            pltpu.VMEM((2, 2, ny, nz, 16, columns // 2), BF16),
            pltpu.VMEM((4 * block_len, columns), BF16),
            pltpu.VMEM((entries, block_len, block_len), BF16),
            pltpu.VMEM((2, block_len, 4 * block_len), BF16),
            pltpu.VMEM((block_len, 4 * block_len), BF16),
            pltpu.VMEM((columns, columns), BF16),
            pltpu.VMEM((columns, columns), BF16),
            pltpu.VMEM((block_len, 2 * columns), BF16),
            pltpu.VMEM((chips, 16, columns // 2), BF16),
            pltpu.VMEM((5 * nz, 16, columns // 2), BF16),
            pltpu.VMEM((2, nz, 16, columns // 2), BF16),
            pltpu.VMEM((2, nz // 2, 16, columns // 2), BF16),
            dma((7,)), dma((2,)), dma((2,)), dma((nz,)), dma((nz,)),
            dma((nz - 1,)), dma((nz - 1,)),
            dma((2, 2, far)), dma((2, 2, far)),
            dma((2, 2 * far + 1)), dma((2, 2 * far + 1)),
            dma((2, 2)), dma((2, 2)),
            dma((5 * nz,)), dma((5 * nz,)),
        ],
        compiler_params=pltpu.CompilerParams(
            collective_id=0, has_side_effects=True, vmem_limit_bytes=64 * 1024 * 1024,
        ),
        name="sigma",
    )(trial, block_rows, right_ops, left_ops, ent_source, ent_target, ent_count.reshape(1, 1))


def solution(mesh):
    nz = 4
    sectors = mesh.shape["sector"]
    ny = mesh.shape["term"] // (2 * nz)
    placed = (
        P(("sector", "term"), None),
        P("sector"),
        P(("sector", "term"), None, None),
        P(("sector", "term"), None, None, None),
        P(("sector", "term"), None),
        P(("sector", "term"), None),
        P(("sector", "term")),
    )
    return jax.shard_map(
        functools.partial(local, sectors, ny, nz), mesh=mesh, in_specs=placed,
        out_specs=P(("sector", "term"), None), check_vma=False,
    )
```

```python
import functools

import jax
import jax.numpy as jnp
from jax import lax
from jax.experimental import pallas as pl
from jax.experimental.pallas import tpu as pltpu
from jax.sharding import PartitionSpec as P

MESH = pl.DeviceIdType.MESH
F32 = jnp.float32
BF16 = jnp.bfloat16
SKIP = True


def kernel(
    sectors, ny, nz,
    trial_in, rows_in, right_ref, left_ref, source_in, target_in, count_in,
    out_ref,
    trial_ref, rows_ref, source_ref, target_ref, count_ref,
    units, window, lefts, weights, weights_sib, right_own, right_sib, projected, outgoing, incoming,
    passed, passed_half, early,
    load_sem, pair_send, pair_recv, next_send, next_recv, o_send, o_recv, z_send, z_recv, y_send, y_recv,
    d_send, d_recv, m_send, m_recv, r_send, r_recv,
):
    entries, block_len = lefts.shape[0], lefts.shape[1]
    columns = right_own.shape[0]
    half = columns // 2
    group_rows = 2 * block_len
    chips = ny * nz
    far = ny // 2
    s = lax.axis_index("sector")
    t = lax.axis_index("term")
    y, z, c = t // (2 * nz), lax.rem(t // 2, nz), lax.rem(t, 2)
    me = t // 2

    def device(sector, chip, core):
        return (sector, chip * 2 + core)

    sibling = device(s, me, 1 - c)
    following = lax.rem(s + 1, sectors)
    preceding = lax.rem(s + sectors - 1, sectors)

    def near(dy, dz):
        return lax.rem(y + dy + ny, ny) * nz + lax.rem(z + dz, nz)


    loads = [
        pltpu.make_async_copy(source, destination, load_sem.at[i])
        for i, (source, destination) in enumerate([
            (trial_in, trial_ref), (rows_in, rows_ref), (source_in, source_ref), (target_in, target_ref),
            (count_in, count_ref), (left_ref.at[0], lefts), (right_ref.at[0], right_own),
        ])
    ]
    for load in loads:
        load.start()

    barrier = pltpu.get_barrier_semaphore()

    def greet(target):
        pl.semaphore_signal(barrier, inc=1, device_id=target, device_id_type=MESH)

    greet(sibling)
    for dz in range(nz):
        greet(device(preceding, near(0, dz), c))
    for dy in range(-2, 3):
        for dz in range(nz):
            if dy or dz:
                greet(device(s, near(dy, dz), c))

    loads[0].wait()
    loads[1].wait()
    start_row = t * 8
    limit = rows_ref[start_row // block_len]
    inside = lax.rem(start_row, block_len) + lax.broadcasted_iota(jnp.int32, (8, columns), 0)
    live_rows = inside < limit
    rows = jnp.where(live_rows, trial_ref[...].astype(F32), 0.0)
    units[0, c, y, z] = jnp.concatenate([rows[:, :half], rows[:, half:]], axis=0).astype(BF16)

    pl.semaphore_wait(barrier, 1 + nz + 5 * nz - 1)

    def remote(source, destination, send, recv, target):
        return pltpu.make_async_remote_copy(
            src_ref=source, dst_ref=destination, send_sem=send, recv_sem=recv,
            device_id=target, device_id_type=MESH,
        )

    sends = []

    def begin(copy):
        copy.start()
        sends.append(copy)
        return copy

    def behind(way, k):
        return lax.rem(y - k + ny, ny) if way == 0 else lax.rem(y + k, ny)

    def toward(way, hops):
        return device(s, near(hops if way == 0 else -hops, 0), c)

    def own_unit(way, k):
        if k < far:
            return units.at[0, c, behind(way, k), z]
        return units.at[0, c, behind(way, k), z, :, pl.ds(way * (half // 2), half // 2)]

    def index(way, k):
        return way * far + k if k else 0

    def own_step(way, k, hops):
        row = behind(way, k - hops)
        slot = units.at[0, c, row, z] if k < far else units.at[0, c, row, z, :, pl.ds(way * (half // 2), half // 2)]
        return remote(slot, slot, o_send.at[way, k - 1], o_recv.at[way, k - 1], toward(way, hops))

    def own_spread(way, k):
        slot = own_unit(way, k)
        return [
            remote(slot, slot, z_send.at[index(way, k), d - 1], z_recv.at[index(way, k), d - 1], device(s, near(0, d), c))
            for d in range(nz - 1, 0, -1)
        ]

    def prior_unit(way, k, d):
        return units.at[1, c, behind(way, k), lax.rem(z - d + nz, nz)]

    def carried(way, k):
        return range(nz) if k < far else range(way * (nz // 2), (way + 1) * (nz // 2))

    def prior_step(way, k, d, hops):
        slot = prior_unit(way, k - hops, d)
        return remote(slot, slot, y_send.at[way, k - 1, d], y_recv.at[way, k - 1, d], toward(way, hops))

    def pair_copy(st, way, k, d=None):
        slot = units.at[st, c, behind(way, k)] if d is None else prior_unit(way, k, d)
        at = index(way, k) if d is None else 2 * far + 1 + d
        return remote(slot, slot, d_send.at[st, at], d_recv.at[st, at], sibling)

    own, prior, spread = {}, {}, {}
    for way in range(2):
        own[way, 2] = begin(own_step(way, 2, 2))
        own[way, 1] = begin(own_step(way, 1, 1))
    next_all = [
        begin(remote(units.at[0, c, y, z], units.at[1, c, y, z], next_send.at[d], next_recv.at[d],
                     device(following, near(0, d), c)))
        for d in range(nz)
    ]
    spread[0, 0] = [begin(copy) for copy in own_spread(0, 0)]
    right_copy = begin(remote(right_ref.at[0], right_sib, pair_send.at[1], pair_recv.at[1], sibling))

    pairs = []

    def begin_pair(st, way, k, d=None):
        pairs.append((st, begin(pair_copy(st, way, k, d))))

    def own_arrival(k):
        for way in range(2):
            own[way, k].wait_recv()
            if k == 2:
                own[way, 3] = begin(own_step(way, 3, 1))
                own[way, far] = begin(own_step(way, far, 2))
            spread[way, k] = [begin(copy) for copy in own_spread(way, k)]

    def own_row(k):
        for way in range(2 if k else 1):
            for copy in spread[way, k]:
                copy.wait_recv()
            if k < far:
                begin_pair(0, way, k)
        if k == far:
            begin_pair(0, 0, k)

    def prior_begin(way, k, d, hops):
        if d in carried(way, k):
            prior[way, k, d] = begin(prior_step(way, k, d, hops))

    def prior_arrival(k):
        for d in range(nz):
            for way in range(2):
                if k == 0:
                    if way == 0:
                        next_all[d].wait_recv()
                    if SKIP:
                        prior_begin(way, 2, d, 2)
                    prior_begin(way, 1, d, 1)
                elif d in carried(way, k):
                    prior[way, k, d].wait_recv()
                    if k == 1 and not SKIP:
                        prior_begin(way, 2, d, 1)
                    if k == 2:
                        prior_begin(way, far, d, 2)
                        prior_begin(way, 3, d, 1)
                    if k == far:
                        begin_pair(1, way, k, d)
        if k < far:
            for way in range(2 if k else 1):
                begin_pair(1, way, k)

    own_arrival(1)
    own_arrival(2)
    prior_arrival(0)

    for load in loads[2:6]:
        load.wait()
    count = count_ref[0, 0]
    factors = []
    for k in range(entries):
        live = k < count
        src, dst = source_ref[0, k], target_ref[0, k]
        for b in range(2):
            for w in range(4):
                on = live & (dst == b) & (src == w)
                if w >= 2:
                    on = on & (s > 0)
                factors.append(jnp.where(on, 1.0, 0.0).astype(F32))

    def weigh(i, carry):
        row = pl.multiple_of(i * 32, 32)
        blocks = [lefts[k, pl.ds(row, 32), :].astype(F32) for k in range(entries)]
        at = pl.multiple_of(i * 16, 16)
        for b in range(2):
            for w in range(4):
                total = blocks[0] * factors[b * 4 + w]
                for k in range(1, entries):
                    total = total + blocks[k] * factors[k * 8 + b * 4 + w]
                total = total.reshape(2, 2, 8, block_len)
                for p in range(2):
                    piece = total[:, p].reshape(16, block_len).astype(BF16)
                    weights[p, pl.ds(b * (block_len // 2) + at, 16), w * block_len:(w + 1) * block_len] = piece
        return carry

    lax.fori_loop(0, block_len // 32, weigh, 0)

    weights_copy = begin(remote(weights.at[1 - c], weights_sib, pair_send.at[0], pair_recv.at[0], sibling))

    own_arrival(3)
    own_arrival(4)
    own_row(0)
    prior_arrival(1)
    own_row(1)
    prior_arrival(2)
    own_row(2)
    own_row(3)
    own_row(4)
    prior_arrival(3)
    prior_arrival(4)

    def lay(st):
        def one(row, carry):
            pieces = [units[st, p, row].astype(F32).reshape(nz, 2, 8, half) for p in range(2)]
            at = pl.multiple_of(st * group_rows + row * (nz * 16), 16)
            for h in range(2):
                both = jnp.concatenate([pieces[0][:, h:h + 1], pieces[1][:, h:h + 1]], axis=1)
                window[pl.ds(at, nz * 16), h * half:(h + 1) * half] = both.reshape(nz * 16, half).astype(BF16)
            return carry

        lax.fori_loop(0, ny, one, 0)

    tile = min(256, half)

    def received(st):
        for which, copy in pairs:
            if which == st:
                copy.wait_recv()

    def left_product(operator, st, n):
        rows = slice(st * group_rows, (st + 1) * group_rows)
        return jnp.dot(operator[:, rows], window[rows, n * tile:(n + 1) * tile], preferred_element_type=F32)

    received(0)
    lay(0)
    weights_copy.wait_recv()
    for n in range(columns // tile):
        early[0, :, n * tile:(n + 1) * tile] = left_product(weights[c], 0, n)
        early[1, :, n * tile:(n + 1) * tile] = left_product(weights_sib[...], 0, n)
    received(1)
    lay(1)
    for n in range(columns // tile):
        at = slice(n * tile, (n + 1) * tile)
        projected[:, at] = (early[0, :, at] + left_product(weights[c], 1, n)).astype(BF16)
        at_sib = slice(columns + n * tile, columns + (n + 1) * tile)
        projected[:, at_sib] = (early[1, :, at] + left_product(weights_sib[...], 1, n)).astype(BF16)
    right_copy.wait_recv()
    loads[6].wait()

    def row_at(dy):
        return lax.rem(y + dy + ny, ny) * nz

    part = half // 2
    merged, finals = {}, []

    def deliver(n, dy, dz):
        chip = near(dy, dz)
        at = (2 + dy) * nz
        finals.append(begin(remote(
            outgoing.at[n, chip], incoming.at[n, at + z],
            r_send.at[n, at + dz], r_recv.at[n, at + dz], device(s, chip, c))))

    for n in range(2):
        both = []
        for h in range(2):
            at = h * half + n * part
            value = jnp.dot(projected[:, :columns], right_own[:, at:at + part], preferred_element_type=F32)
            value = value + jnp.dot(projected[:, columns:], right_sib[:, at:at + part], preferred_element_type=F32)
            both.append(value.reshape(chips, 8, part))
        outgoing[n] = jnp.concatenate(both, axis=1).astype(BF16)
        for way, sign in ((0, 1), (1, -1)):
            merged[n, way] = (
                begin(remote(outgoing.at[n, pl.ds(row_at(4) + way * (nz // 2), nz // 2)], passed_half.at[n, way],
                             m_send.at[n, way, 1], m_recv.at[n, way, 1], device(s, near(2 * sign, 0), c))),
                begin(remote(outgoing.at[n, pl.ds(row_at(3 * sign), nz)], passed.at[n, way],
                             m_send.at[n, way, 0], m_recv.at[n, way, 0], device(s, near(sign, 0), c))),
            )

    for n in range(2):
        for dy in (1, -1, 0):
            for dz in range(nz - 1, -1, -1):
                if dy or dz:
                    deliver(n, dy, dz)
        incoming[n, 2 * nz + z] = outgoing[n, me]
    for n in range(2):
        for way, sign in ((0, 1), (1, -1)):
            for copy in merged[n, way]:
                copy.wait_recv()
            for i in range(nz):
                at = row_at(2 * sign) + i
                value = outgoing[n, at].astype(F32) + passed[n, way, i].astype(F32)
                if i // (nz // 2) == way:
                    value = value + passed_half[n, way, i % (nz // 2)].astype(F32)
                outgoing[n, at] = value.astype(BF16)
            for dz in range(nz - 1, -1, -1):
                deliver(n, 2 * sign, dz)

    for copy in finals:
        copy.wait_recv()
    for n in range(2):
        total = incoming[n, 0].astype(F32)
        for i in range(1, 5 * nz):
            total = total + incoming[n, i].astype(F32)
        for h in range(2):
            at = h * half + n * part
            out_ref[:, at:at + part] = jnp.where(
                live_rows[:, :part], total[h * 8:(h + 1) * 8], 0.0).astype(BF16)

    for copy in sends:
        copy.wait_send()


def local(sectors, ny, nz, trial, block_rows, right_ops, left_ops, ent_source, ent_target, ent_count):
    entries, block_len = left_ops.shape[1:3]
    columns = trial.shape[1]
    chips = ny * nz
    far = ny // 2
    dma = pltpu.SemaphoreType.DMA
    vmem = pl.BlockSpec(memory_space=pltpu.VMEM)
    hbm = pl.BlockSpec(memory_space=pl.ANY)
    return pl.pallas_call(
        functools.partial(kernel, sectors, ny, nz),
        out_shape=jax.ShapeDtypeStruct(trial.shape, trial.dtype),
        in_specs=[hbm] * 7,
        out_specs=vmem,
        scratch_shapes=[
            pltpu.VMEM(trial.shape, trial.dtype),
            pltpu.SMEM(block_rows.shape, jnp.int32),
            pltpu.SMEM(ent_source.shape, jnp.int32),
            pltpu.SMEM(ent_target.shape, jnp.int32),
            pltpu.SMEM((1, 1), jnp.int32),
            pltpu.VMEM((2, 2, ny, nz, 16, columns // 2), BF16),
            pltpu.VMEM((4 * block_len, columns), BF16),
            pltpu.VMEM((entries, block_len, block_len), BF16),
            pltpu.VMEM((2, block_len, 4 * block_len), BF16),
            pltpu.VMEM((block_len, 4 * block_len), BF16),
            pltpu.VMEM((columns, columns), BF16),
            pltpu.VMEM((columns, columns), BF16),
            pltpu.VMEM((block_len, 2 * columns), BF16),
            pltpu.VMEM((2, chips, 16, columns // 4), BF16),
            pltpu.VMEM((2, 5 * nz, 16, columns // 4), BF16),
            pltpu.VMEM((2, 2, nz, 16, columns // 4), BF16),
            pltpu.VMEM((2, 2, nz // 2, 16, columns // 4), BF16),
            pltpu.VMEM((2, block_len, columns), F32),
            dma((7,)), dma((2,)), dma((2,)), dma((nz,)), dma((nz,)),
            dma((2, far)), dma((2, far)),
            dma((2 * far + 1, nz - 1)), dma((2 * far + 1, nz - 1)),
            dma((2, far, nz)), dma((2, far, nz)),
            dma((2, 2 * far + 1 + nz)), dma((2, 2 * far + 1 + nz)),
            dma((2, 2, 2)), dma((2, 2, 2)),
            dma((2, 5 * nz)), dma((2, 5 * nz)),
        ],
        compiler_params=pltpu.CompilerParams(
            collective_id=0, has_side_effects=True, vmem_limit_bytes=64 * 1024 * 1024,
        ),
        name="sigma",
    )(trial, block_rows, right_ops, left_ops, ent_source, ent_target, ent_count.reshape(1, 1))


def solution(mesh):
    nz = 4
    sectors = mesh.shape["sector"]
    ny = mesh.shape["term"] // (2 * nz)
    placed = (
        P(("sector", "term"), None),
        P("sector"),
        P(("sector", "term"), None, None),
        P(("sector", "term"), None, None, None),
        P(("sector", "term"), None),
        P(("sector", "term"), None),
        P(("sector", "term")),
    )
    return jax.shard_map(
        functools.partial(local, sectors, ny, nz), mesh=mesh, in_specs=placed,
        out_specs=P(("sector", "term"), None), check_vma=False,
    )
```

```python
import functools

import jax
import jax.numpy as jnp
from jax import lax
from jax.experimental import pallas as pl
from jax.experimental.pallas import tpu as pltpu
from jax.sharding import PartitionSpec as P

MESH = pl.DeviceIdType.MESH
F32 = jnp.float32
BF16 = jnp.bfloat16


def kernel(
    sectors, ny, nz,
    trial_in, rows_in, right_ref, left_ref, source_in, target_in, count_in,
    out_ref,
    trial_ref, rows_ref, source_ref, target_ref, count_ref,
    units, window, lefts, weights, weights_sib, right_own, right_sib, projected, outgoing, incoming,
    passed, passed_half, early,
    load_sem, pair_send, pair_recv, next_send, next_recv, o_send, o_recv, z_send, z_recv, y_send, y_recv,
    d_send, d_recv, m_send, m_recv, r_send, r_recv,
):
    entries, block_len = lefts.shape[0], lefts.shape[1]
    columns = right_own.shape[0]
    half = columns // 2
    group_rows = 2 * block_len
    chips = ny * nz
    far = ny // 2
    s = lax.axis_index("sector")
    t = lax.axis_index("term")
    y, z, c = t // (2 * nz), lax.rem(t // 2, nz), lax.rem(t, 2)
    me = t // 2

    def device(sector, chip, core):
        return (sector, chip * 2 + core)

    sibling = device(s, me, 1 - c)
    following = lax.rem(s + 1, sectors)
    preceding = lax.rem(s + sectors - 1, sectors)

    def near(dy, dz):
        return lax.rem(y + dy + ny, ny) * nz + lax.rem(z + dz, nz)


    loads = [
        pltpu.make_async_copy(source, destination, load_sem.at[i])
        for i, (source, destination) in enumerate([
            (trial_in, trial_ref), (rows_in, rows_ref), (source_in, source_ref), (target_in, target_ref),
            (count_in, count_ref), (left_ref.at[0], lefts), (right_ref.at[0], right_own),
        ])
    ]
    for load in loads:
        load.start()

    barrier = pltpu.get_barrier_semaphore()

    def greet(target):
        pl.semaphore_signal(barrier, inc=1, device_id=target, device_id_type=MESH)

    greet(sibling)

    @pl.when(s > 0)
    def _():
        for dz in range(nz):
            greet(device(preceding, near(0, dz), c))

    for dy in range(-2, 3):
        for dz in range(nz):
            if dy or dz:
                greet(device(s, near(dy, dz), c))

    loads[0].wait()
    loads[1].wait()
    start_row = t * 8
    limit = rows_ref[start_row // block_len]
    inside = lax.rem(start_row, block_len) + lax.broadcasted_iota(jnp.int32, (8, columns), 0)
    live_rows = inside < limit
    rows = jnp.where(live_rows, trial_ref[...].astype(F32), 0.0)
    units[0, c, y, z] = jnp.concatenate([rows[:, :half], rows[:, half:]], axis=0).astype(BF16)

    @pl.when(s < sectors - 1)
    def _():
        pl.semaphore_wait(barrier, 6 * nz)

    @pl.when(s == sectors - 1)
    def _():
        pl.semaphore_wait(barrier, 5 * nz)


    def remote(source, destination, send, recv, target):
        return pltpu.make_async_remote_copy(
            src_ref=source, dst_ref=destination, send_sem=send, recv_sem=recv,
            device_id=target, device_id_type=MESH,
        )

    sends = []

    def begin(copy):
        copy.start()
        sends.append(copy)
        return copy

    def behind(way, k):
        return lax.rem(y - k + ny, ny) if way == 0 else lax.rem(y + k, ny)

    def toward(way, hops):
        return device(s, near(hops if way == 0 else -hops, 0), c)

    def own_unit(way, k):
        if k < far:
            return units.at[0, c, behind(way, k), z]
        return units.at[0, c, behind(way, k), z, :, pl.ds(way * (half // 2), half // 2)]

    def index(way, k):
        return way * far + k if k else 0

    def own_step(way, k, hops):
        row = behind(way, k - hops)
        slot = units.at[0, c, row, z] if k < far else units.at[0, c, row, z, :, pl.ds(way * (half // 2), half // 2)]
        return remote(slot, slot, o_send.at[way, k - 1], o_recv.at[way, k - 1], toward(way, hops))

    def own_spread(way, k):
        slot = own_unit(way, k)
        return [
            remote(slot, slot, z_send.at[index(way, k), d - 1], z_recv.at[index(way, k), d - 1], device(s, near(0, d), c))
            for d in range(nz - 1, 0, -1)
        ]

    def prior_unit(way, k, d):
        return units.at[1, c, behind(way, k), lax.rem(z - d + nz, nz)]

    def carried(way, k):
        return range(nz) if k < far else range(way * (nz // 2), (way + 1) * (nz // 2))

    def prior_step(way, k, d, hops):
        slot = prior_unit(way, k - hops, d)
        return remote(slot, slot, y_send.at[way, k - 1, d], y_recv.at[way, k - 1, d], toward(way, hops))

    def pair_copy(st, way, k, d=None):
        slot = units.at[st, c, behind(way, k)] if d is None else prior_unit(way, k, d)
        at = index(way, k) if d is None else 2 * far + 1 + d
        return remote(slot, slot, d_send.at[st, at], d_recv.at[st, at], sibling)

    own, spread = {}, {}
    for way in range(2):
        own[way, 2] = begin(own_step(way, 2, 2))
        own[way, 1] = begin(own_step(way, 1, 1))
    next_all = [
        remote(units.at[0, c, y, z], units.at[1, c, y, z], next_send.at[d], next_recv.at[d],
               device(following, near(0, d), c))
        for d in range(nz)
    ]

    @pl.when(s < sectors - 1)
    def _():
        for copy in next_all:
            copy.start()

    spread[0, 0] = [begin(copy) for copy in own_spread(0, 0)]

    pairs = []

    prior = {
        (way, k, d): prior_step(way, k, d, 2 if k in (2, far) else 1)
        for k in range(1, far + 1) for way in range(2) for d in carried(way, k)
    }
    prior_pairs = {(0, 0): [pair_copy(1, 0, 0)]}
    for k in range(1, far):
        for way in range(2):
            prior_pairs[way, k] = [pair_copy(1, way, k)]
    for way in range(2):
        prior_pairs[way, far] = [pair_copy(1, way, far, d) for d in carried(way, far)]

    def begin_pair(way, k):
        pairs.append(begin(pair_copy(0, way, k)))

    def own_arrival(k):
        for way in range(2):
            own[way, k].wait_recv()
            if k == 2:
                own[way, 3] = begin(own_step(way, 3, 1))
                own[way, far] = begin(own_step(way, far, 2))
            spread[way, k] = [begin(copy) for copy in own_spread(way, k)]

    def own_row(k):
        for way in range(2 if k else 1):
            for copy in spread[way, k]:
                copy.wait_recv()
            if k < far:
                begin_pair(way, k)
        if k == far:
            begin_pair(0, k)

    def prior_arrival(k):
        @pl.when(s > 0)
        def _():
            for d in range(nz):
                if k == 0:
                    next_all[d].wait_recv()
                for way in range(2):
                    if k == 0:
                        prior[way, 2, d].start()
                        prior[way, 1, d].start()
                    elif d in carried(way, k):
                        prior[way, k, d].wait_recv()
                        if k == 2:
                            if d in carried(way, far):
                                prior[way, far, d].start()
                            prior[way, 3, d].start()
                        if k == far:
                            prior_pairs[way, far][d - carried(way, far)[0]].start()
            if k < far:
                for way in range(2 if k else 1):
                    prior_pairs[way, k][0].start()

    own_arrival(1)
    own_arrival(2)
    prior_arrival(0)

    for load in loads[2:6]:
        load.wait()
    count = count_ref[0, 0]
    factors = []
    for k in range(entries):
        live = k < count
        src, dst = source_ref[0, k], target_ref[0, k]
        for b in range(2):
            for w in range(4):
                on = live & (dst == b) & (src == w)
                if w >= 2:
                    on = on & (s > 0)
                factors.append(jnp.where(on, 1.0, 0.0).astype(F32))

    def weigh(i, carry):
        row = pl.multiple_of(i * 32, 32)
        blocks = [lefts[k, pl.ds(row, 32), :].astype(F32) for k in range(entries)]
        at = pl.multiple_of(i * 16, 16)
        for b in range(2):
            for w in range(4):
                total = blocks[0] * factors[b * 4 + w]
                for k in range(1, entries):
                    total = total + blocks[k] * factors[k * 8 + b * 4 + w]
                total = total.reshape(2, 2, 8, block_len)
                for p in range(2):
                    piece = total[:, p].reshape(16, block_len).astype(BF16)
                    weights[p, pl.ds(b * (block_len // 2) + at, 16), w * block_len:(w + 1) * block_len] = piece
        return carry

    lax.fori_loop(0, block_len // 32, weigh, 0)

    right_copy = begin(remote(right_ref.at[0], right_sib, pair_send.at[1], pair_recv.at[1], sibling))
    weights_copy = begin(remote(weights.at[1 - c], weights_sib, pair_send.at[0], pair_recv.at[0], sibling))

    own_arrival(3)
    own_arrival(4)
    own_row(0)
    prior_arrival(1)
    own_row(1)
    prior_arrival(2)
    own_row(2)
    own_row(3)
    own_row(4)
    prior_arrival(3)
    prior_arrival(4)

    def lay(st):
        def one(row, carry):
            pieces = [units[st, p, row].astype(F32).reshape(nz, 2, 8, half) for p in range(2)]
            at = pl.multiple_of(st * group_rows + row * (nz * 16), 16)
            for h in range(2):
                both = jnp.concatenate([pieces[0][:, h:h + 1], pieces[1][:, h:h + 1]], axis=1)
                window[pl.ds(at, nz * 16), h * half:(h + 1) * half] = both.reshape(nz * 16, half).astype(BF16)
            return carry

        lax.fori_loop(0, ny, one, 0)

    tile = min(256, half)

    def left_product(operator, st, n):
        rows = slice(st * group_rows, (st + 1) * group_rows)
        return jnp.dot(operator[:, rows], window[rows, n * tile:(n + 1) * tile], preferred_element_type=F32)

    for copy in pairs:
        copy.wait_recv()
    lay(0)
    weights_copy.wait_recv()
    for n in range(columns // tile):
        early[0, :, n * tile:(n + 1) * tile] = left_product(weights[c], 0, n)
        early[1, :, n * tile:(n + 1) * tile] = left_product(weights_sib[...], 0, n)

    @pl.when(s > 0)
    def _():
        for copies in prior_pairs.values():
            for copy in copies:
                copy.wait_recv()
        lay(1)

    @pl.when(s == 0)
    def _():
        window[group_rows:, :] = jnp.zeros((group_rows, columns), BF16)

    for n in range(columns // tile):
        at = slice(n * tile, (n + 1) * tile)
        projected[:, at] = (early[0, :, at] + left_product(weights[c], 1, n)).astype(BF16)
        at_sib = slice(columns + n * tile, columns + (n + 1) * tile)
        projected[:, at_sib] = (early[1, :, at] + left_product(weights_sib[...], 1, n)).astype(BF16)
    right_copy.wait_recv()
    loads[6].wait()

    def row_at(dy):
        return lax.rem(y + dy + ny, ny) * nz

    part = half // 2
    merged, finals = {}, []

    def deliver(n, dy, dz):
        chip = near(dy, dz)
        at = (2 + dy) * nz
        finals.append(begin(remote(
            outgoing.at[n, chip], incoming.at[n, at + z],
            r_send.at[n, at + dz], r_recv.at[n, at + dz], device(s, chip, c))))

    for n in range(2):
        both = []
        for h in range(2):
            at = h * half + n * part
            value = jnp.dot(projected[:, :columns], right_own[:, at:at + part], preferred_element_type=F32)
            value = value + jnp.dot(projected[:, columns:], right_sib[:, at:at + part], preferred_element_type=F32)
            both.append(value.reshape(chips, 8, part))
        outgoing[n] = jnp.concatenate(both, axis=1).astype(BF16)
        for way, sign in ((0, 1), (1, -1)):
            merged[n, way] = (
                begin(remote(outgoing.at[n, pl.ds(row_at(4) + way * (nz // 2), nz // 2)], passed_half.at[n, way],
                             m_send.at[n, way, 1], m_recv.at[n, way, 1], device(s, near(2 * sign, 0), c))),
                begin(remote(outgoing.at[n, pl.ds(row_at(3 * sign), nz)], passed.at[n, way],
                             m_send.at[n, way, 0], m_recv.at[n, way, 0], device(s, near(sign, 0), c))),
            )

    for n in range(2):
        for dy in (1, -1, 0):
            for dz in range(nz - 1, -1, -1):
                if dy or dz:
                    deliver(n, dy, dz)
        incoming[n, 2 * nz + z] = outgoing[n, me]
    for n in range(2):
        for way, sign in ((0, 1), (1, -1)):
            for copy in merged[n, way]:
                copy.wait_recv()
            for i in range(nz):
                at = row_at(2 * sign) + i
                value = outgoing[n, at].astype(F32) + passed[n, way, i].astype(F32)
                if i // (nz // 2) == way:
                    value = value + passed_half[n, way, i % (nz // 2)].astype(F32)
                outgoing[n, at] = value.astype(BF16)
            for dz in range(nz - 1, -1, -1):
                deliver(n, 2 * sign, dz)

    early_sends = len(sends) - 4 * nz
    for copy in sends[:early_sends]:
        copy.wait_send()

    @pl.when(s > 0)
    def _():
        for copy in prior.values():
            copy.wait_send()
        for copies in prior_pairs.values():
            for copy in copies:
                copy.wait_send()

    @pl.when(s < sectors - 1)
    def _():
        for copy in next_all:
            copy.wait_send()

    for copy in finals:
        copy.wait_recv()
    for n in range(2):
        total = incoming[n, 0].astype(F32)
        for i in range(1, 5 * nz):
            total = total + incoming[n, i].astype(F32)
        for h in range(2):
            at = h * half + n * part
            out_ref[:, at:at + part] = jnp.where(
                live_rows[:, :part], total[h * 8:(h + 1) * 8], 0.0).astype(BF16)

    for copy in sends[early_sends:]:
        copy.wait_send()


def local(sectors, ny, nz, trial, block_rows, right_ops, left_ops, ent_source, ent_target, ent_count):
    entries, block_len = left_ops.shape[1:3]
    columns = trial.shape[1]
    chips = ny * nz
    far = ny // 2
    dma = pltpu.SemaphoreType.DMA
    vmem = pl.BlockSpec(memory_space=pltpu.VMEM)
    hbm = pl.BlockSpec(memory_space=pl.ANY)
    return pl.pallas_call(
        functools.partial(kernel, sectors, ny, nz),
        out_shape=jax.ShapeDtypeStruct(trial.shape, trial.dtype),
        in_specs=[hbm] * 7,
        out_specs=vmem,
        scratch_shapes=[
            pltpu.VMEM(trial.shape, trial.dtype),
            pltpu.SMEM(block_rows.shape, jnp.int32),
            pltpu.SMEM(ent_source.shape, jnp.int32),
            pltpu.SMEM(ent_target.shape, jnp.int32),
            pltpu.SMEM((1, 1), jnp.int32),
            pltpu.VMEM((2, 2, ny, nz, 16, columns // 2), BF16),
            pltpu.VMEM((4 * block_len, columns), BF16),
            pltpu.VMEM((entries, block_len, block_len), BF16),
            pltpu.VMEM((2, block_len, 4 * block_len), BF16),
            pltpu.VMEM((block_len, 4 * block_len), BF16),
            pltpu.VMEM((columns, columns), BF16),
            pltpu.VMEM((columns, columns), BF16),
            pltpu.VMEM((block_len, 2 * columns), BF16),
            pltpu.VMEM((2, chips, 16, columns // 4), BF16),
            pltpu.VMEM((2, 5 * nz, 16, columns // 4), BF16),
            pltpu.VMEM((2, 2, nz, 16, columns // 4), BF16),
            pltpu.VMEM((2, 2, nz // 2, 16, columns // 4), BF16),
            pltpu.VMEM((2, block_len, columns), F32),
            dma((7,)), dma((2,)), dma((2,)), dma((nz,)), dma((nz,)),
            dma((2, far)), dma((2, far)),
            dma((2 * far + 1, nz - 1)), dma((2 * far + 1, nz - 1)),
            dma((2, far, nz)), dma((2, far, nz)),
            dma((2, 2 * far + 1 + nz)), dma((2, 2 * far + 1 + nz)),
            dma((2, 2, 2)), dma((2, 2, 2)),
            dma((2, 5 * nz)), dma((2, 5 * nz)),
        ],
        compiler_params=pltpu.CompilerParams(
            collective_id=0, has_side_effects=True, vmem_limit_bytes=64 * 1024 * 1024,
        ),
        name="sigma",
    )(trial, block_rows, right_ops, left_ops, ent_source, ent_target, ent_count.reshape(1, 1))


def solution(mesh):
    nz = 4
    sectors = mesh.shape["sector"]
    ny = mesh.shape["term"] // (2 * nz)
    placed = (
        P(("sector", "term"), None),
        P("sector"),
        P(("sector", "term"), None, None),
        P(("sector", "term"), None, None, None),
        P(("sector", "term"), None),
        P(("sector", "term"), None),
        P(("sector", "term")),
    )
    return jax.shard_map(
        functools.partial(local, sectors, ny, nz), mesh=mesh, in_specs=placed,
        out_specs=P(("sector", "term"), None), check_vma=False,
    )
```

```python
import functools

import jax
import jax.numpy as jnp
from jax import lax
from jax.experimental import pallas as pl
from jax.experimental.pallas import tpu as pltpu
from jax.sharding import PartitionSpec as P

MESH = pl.DeviceIdType.MESH
F32 = jnp.float32
BF16 = jnp.bfloat16


def kernel(
    sectors, ny, nz,
    trial_in, rows_in, right_ref, left_ref, source_in, target_in, count_in,
    out_ref,
    trial_ref, rows_ref, source_ref, target_ref, count_ref,
    units, window, lefts, weights, weights_sib, right_own, right_sib, projected, outgoing, incoming,
    passed, passed_half, early,
    load_sem, pair_send, pair_recv, next_send, next_recv, o_send, o_recv, z_send, z_recv, y_send, y_recv,
    d_send, d_recv, m_send, m_recv, r_send, r_recv,
):
    entries, block_len = lefts.shape[0], lefts.shape[1]
    columns = right_own.shape[0]
    half = columns // 2
    group_rows = 2 * block_len
    chips = ny * nz
    far = ny // 2
    s = lax.axis_index("sector")
    t = lax.axis_index("term")
    y, z, c = t // (2 * nz), lax.rem(t // 2, nz), lax.rem(t, 2)
    me = t // 2

    def device(sector, chip, core):
        return (sector, chip * 2 + core)

    sibling = device(s, me, 1 - c)
    following = lax.rem(s + 1, sectors)
    preceding = lax.rem(s + sectors - 1, sectors)

    def near(dy, dz):
        return lax.rem(y + dy + ny, ny) * nz + lax.rem(z + dz, nz)


    loads = [
        pltpu.make_async_copy(source, destination, load_sem.at[i])
        for i, (source, destination) in enumerate([
            (trial_in, trial_ref), (rows_in, rows_ref), (source_in, source_ref), (target_in, target_ref),
            (count_in, count_ref), (left_ref.at[0], lefts), (right_ref.at[0], right_own),
        ])
    ]
    for load in loads:
        load.start()

    barrier = pltpu.get_barrier_semaphore()

    def greet(target):
        pl.semaphore_signal(barrier, inc=1, device_id=target, device_id_type=MESH)

    greet(sibling)

    @pl.when(s > 0)
    def _():
        for dz in range(nz):
            greet(device(preceding, near(0, dz), c))

    for dy in range(-2, 3):
        for dz in range(nz):
            if dy or dz:
                greet(device(s, near(dy, dz), c))

    loads[0].wait()
    loads[1].wait()
    start_row = t * 8
    limit = rows_ref[start_row // block_len]
    inside = lax.rem(start_row, block_len) + lax.broadcasted_iota(jnp.int32, (8, columns), 0)
    live_rows = inside < limit
    rows = jnp.where(live_rows, trial_ref[...].astype(F32), 0.0)
    units[0, c, y, z] = jnp.concatenate([rows[:, :half], rows[:, half:]], axis=0).astype(BF16)

    @pl.when(s < sectors - 1)
    def _():
        pl.semaphore_wait(barrier, 6 * nz)

    @pl.when(s == sectors - 1)
    def _():
        pl.semaphore_wait(barrier, 5 * nz)


    def remote(source, destination, send, recv, target):
        return pltpu.make_async_remote_copy(
            src_ref=source, dst_ref=destination, send_sem=send, recv_sem=recv,
            device_id=target, device_id_type=MESH,
        )

    sends = []

    def begin(copy):
        copy.start()
        sends.append(copy)
        return copy

    def behind(way, k):
        return lax.rem(y - k + ny, ny) if way == 0 else lax.rem(y + k, ny)

    def toward(way, hops):
        return device(s, near(hops if way == 0 else -hops, 0), c)

    def own_unit(way, k):
        if k < far:
            return units.at[0, c, behind(way, k), z]
        return units.at[0, c, behind(way, k), z, :, pl.ds(way * (half // 2), half // 2)]

    def index(way, k):
        return way * far + k if k else 0

    def own_step(way, k, hops):
        row = behind(way, k - hops)
        slot = units.at[0, c, row, z] if k < far else units.at[0, c, row, z, :, pl.ds(way * (half // 2), half // 2)]
        return remote(slot, slot, o_send.at[way, k - 1], o_recv.at[way, k - 1], toward(way, hops))

    def own_spread(way, k):
        slot = own_unit(way, k)
        return [
            remote(slot, slot, z_send.at[index(way, k), d - 1], z_recv.at[index(way, k), d - 1], device(s, near(0, d), c))
            for d in range(nz - 1, 0, -1)
        ]

    def prior_unit(way, k, d):
        return units.at[1, c, behind(way, k), lax.rem(z - d + nz, nz)]

    def carried(way, k):
        return range(nz) if k < far else range(way * (nz // 2), (way + 1) * (nz // 2))

    def prior_step(way, k, d, hops):
        slot = prior_unit(way, k - hops, d)
        return remote(slot, slot, y_send.at[way, k - 1, d], y_recv.at[way, k - 1, d], toward(way, hops))

    def pair_copy(st, way, k, d=None):
        slot = units.at[st, c, behind(way, k)] if d is None else prior_unit(way, k, d)
        at = index(way, k) if d is None else 2 * far + 1 + d
        return remote(slot, slot, d_send.at[st, at], d_recv.at[st, at], sibling)

    own, spread = {}, {}
    for way in range(2):
        own[way, 2] = begin(own_step(way, 2, 2))
        own[way, 1] = begin(own_step(way, 1, 1))
    next_all = [
        remote(units.at[0, c, y, z], units.at[1, c, y, z], next_send.at[d], next_recv.at[d],
               device(following, near(0, d), c))
        for d in range(nz)
    ]

    @pl.when(s < sectors - 1)
    def _():
        for copy in next_all:
            copy.start()

    spread[0, 0] = [begin(copy) for copy in own_spread(0, 0)]

    pairs = []

    prior = {
        (way, k, d): prior_step(way, k, d, 2 if k in (2, far) else 1)
        for k in range(1, far + 1) for way in range(2) for d in carried(way, k)
    }
    prior_pairs = {(0, 0): [pair_copy(1, 0, 0)]}
    for k in range(1, far):
        for way in range(2):
            prior_pairs[way, k] = [pair_copy(1, way, k)]
    for way in range(2):
        prior_pairs[way, far] = [pair_copy(1, way, far, d) for d in carried(way, far)]

    def begin_pair(way, k):
        pairs.append(begin(pair_copy(0, way, k)))

    def own_arrival(k):
        for way in range(2):
            own[way, k].wait_recv()
            if k == 2:
                own[way, 3] = begin(own_step(way, 3, 1))
                own[way, far] = begin(own_step(way, far, 2))
            spread[way, k] = [begin(copy) for copy in own_spread(way, k)]

    def own_row(k):
        for way in range(2 if k else 1):
            for copy in spread[way, k]:
                copy.wait_recv()
            if k < far:
                begin_pair(way, k)
        if k == far:
            begin_pair(0, k)

    def prior_arrival(k):
        @pl.when(s > 0)
        def _():
            for d in range(nz):
                if k == 0:
                    next_all[d].wait_recv()
                for way in range(2):
                    if k == 0:
                        prior[way, 2, d].start()
                        prior[way, 1, d].start()
                    elif d in carried(way, k):
                        prior[way, k, d].wait_recv()
                        if k == 2:
                            if d in carried(way, far):
                                prior[way, far, d].start()
                            prior[way, 3, d].start()
                        if k == far:
                            prior_pairs[way, far][d - carried(way, far)[0]].start()
            if k < far:
                for way in range(2 if k else 1):
                    prior_pairs[way, k][0].start()

    own_arrival(1)
    own_arrival(2)
    prior_arrival(0)

    for load in loads[2:6]:
        load.wait()
    count = count_ref[0, 0]
    factors = []
    for k in range(entries):
        live = k < count
        src, dst = source_ref[0, k], target_ref[0, k]
        for b in range(2):
            for w in range(4):
                on = live & (dst == b) & (src == w)
                if w >= 2:
                    on = on & (s > 0)
                factors.append(jnp.where(on, 1.0, 0.0).astype(F32))

    def weigh(i, carry):
        row = pl.multiple_of(i * 32, 32)
        blocks = [lefts[k, pl.ds(row, 32), :].astype(F32) for k in range(entries)]
        at = pl.multiple_of(i * 16, 16)
        for b in range(2):
            for w in range(4):
                total = blocks[0] * factors[b * 4 + w]
                for k in range(1, entries):
                    total = total + blocks[k] * factors[k * 8 + b * 4 + w]
                total = total.reshape(2, 2, 8, block_len)
                for p in range(2):
                    piece = total[:, p].reshape(16, block_len).astype(BF16)
                    weights[p, pl.ds(b * (block_len // 2) + at, 16), w * block_len:(w + 1) * block_len] = piece
        return carry

    lax.fori_loop(0, block_len // 32, weigh, 0)

    right_copy = begin(remote(right_ref.at[0], right_sib, pair_send.at[1], pair_recv.at[1], sibling))
    weights_copy = begin(remote(weights.at[1 - c], weights_sib, pair_send.at[0], pair_recv.at[0], sibling))

    own_arrival(3)
    own_arrival(4)
    own_row(0)
    prior_arrival(1)
    own_row(1)
    prior_arrival(2)
    own_row(2)
    own_row(3)
    own_row(4)
    prior_arrival(3)
    prior_arrival(4)

    def lay(st):
        def one(row, carry):
            pieces = [units[st, p, row].astype(F32).reshape(nz, 2, 8, half) for p in range(2)]
            at = pl.multiple_of(st * group_rows + row * (nz * 16), 16)
            for h in range(2):
                both = jnp.concatenate([pieces[0][:, h:h + 1], pieces[1][:, h:h + 1]], axis=1)
                window[pl.ds(at, nz * 16), h * half:(h + 1) * half] = both.reshape(nz * 16, half).astype(BF16)
            return carry

        lax.fori_loop(0, ny, one, 0)

    tile = min(256, half)

    def left_product(operator, st, n):
        rows = slice(st * group_rows, (st + 1) * group_rows)
        return jnp.dot(operator[:, rows], window[rows, n * tile:(n + 1) * tile], preferred_element_type=F32)

    for copy in pairs:
        copy.wait_recv()
    lay(0)
    weights_copy.wait_recv()
    for n in range(columns // tile):
        early[0, :, n * tile:(n + 1) * tile] = left_product(weights[c], 0, n)
        early[1, :, n * tile:(n + 1) * tile] = left_product(weights_sib[...], 0, n)

    @pl.when(s > 0)
    def _():
        for copies in prior_pairs.values():
            for copy in copies:
                copy.wait_recv()
        lay(1)

    @pl.when(s == 0)
    def _():
        window[group_rows:, :] = jnp.zeros((group_rows, columns), BF16)

    for n in range(columns // tile):
        at = slice(n * tile, (n + 1) * tile)
        projected[:, at] = (early[0, :, at] + left_product(weights[c], 1, n)).astype(BF16)
        at_sib = slice(columns + n * tile, columns + (n + 1) * tile)
        projected[:, at_sib] = (early[1, :, at] + left_product(weights_sib[...], 1, n)).astype(BF16)
    right_copy.wait_recv()
    loads[6].wait()

    def row_at(dy):
        return lax.rem(y + dy + ny, ny) * nz

    part = half // 2
    merged, finals = {}, []

    def deliver(n, dy, dz):
        chip = near(dy, dz)
        at = (2 + dy) * nz
        finals.append(begin(remote(
            outgoing.at[n, chip], incoming.at[n, at + z],
            r_send.at[n, at + dz], r_recv.at[n, at + dz], device(s, chip, c))))

    for n in range(2):
        both = []
        for h in range(2):
            at = h * half + n * part
            value = jnp.dot(projected[:, :columns], right_own[:, at:at + part], preferred_element_type=F32)
            value = value + jnp.dot(projected[:, columns:], right_sib[:, at:at + part], preferred_element_type=F32)
            both.append(value.reshape(chips, 8, part))
        outgoing[n] = jnp.concatenate(both, axis=1).astype(BF16)
        for way, sign in ((0, 1), (1, -1)):
            merged[n, way] = (
                begin(remote(outgoing.at[n, pl.ds(row_at(4) + way * (nz // 2), nz // 2)], passed_half.at[n, way],
                             m_send.at[n, way, 1], m_recv.at[n, way, 1], device(s, near(2 * sign, 0), c))),
                begin(remote(outgoing.at[n, pl.ds(row_at(3 * sign), nz)], passed.at[n, way],
                             m_send.at[n, way, 0], m_recv.at[n, way, 0], device(s, near(sign, 0), c))),
            )

    for n in range(2):
        for dy in (1, -1, 0):
            for dz in range(nz - 1, -1, -1):
                if dy or dz:
                    deliver(n, dy, dz)
        incoming[n, 2 * nz + z] = outgoing[n, me]
    for n in range(2):
        for way, sign in ((0, 1), (1, -1)):
            for copy in merged[n, way]:
                copy.wait_recv()
            for i in range(nz):
                at = row_at(2 * sign) + i
                value = outgoing[n, at].astype(F32) + passed[n, way, i].astype(F32)
                if i // (nz // 2) == way:
                    value = value + passed_half[n, way, i % (nz // 2)].astype(F32)
                outgoing[n, at] = value.astype(BF16)
            for dz in range(nz - 1, -1, -1):
                deliver(n, 2 * sign, dz)

    early_sends = len(sends) - 4 * nz
    for copy in sends[:early_sends]:
        copy.wait_send()

    @pl.when(s > 0)
    def _():
        for copy in prior.values():
            copy.wait_send()
        for copies in prior_pairs.values():
            for copy in copies:
                copy.wait_send()

    @pl.when(s < sectors - 1)
    def _():
        for copy in next_all:
            copy.wait_send()

    for copy in finals:
        copy.wait_recv()
    for n in range(2):
        total = incoming[n, 0].astype(F32)
        for i in range(1, 5 * nz):
            total = total + incoming[n, i].astype(F32)
        for h in range(2):
            at = h * half + n * part
            out_ref[:, at:at + part] = jnp.where(
                live_rows[:, :part], total[h * 8:(h + 1) * 8], 0.0).astype(BF16)

    for copy in sends[early_sends:]:
        copy.wait_send()


def local(sectors, ny, nz, trial, block_rows, right_ops, left_ops, ent_source, ent_target, ent_count):
    entries, block_len = left_ops.shape[1:3]
    columns = trial.shape[1]
    chips = ny * nz
    far = ny // 2
    dma = pltpu.SemaphoreType.DMA
    vmem = pl.BlockSpec(memory_space=pltpu.VMEM)
    hbm = pl.BlockSpec(memory_space=pl.ANY)
    return pl.pallas_call(
        functools.partial(kernel, sectors, ny, nz),
        out_shape=pltpu.VMEM(trial.shape, trial.dtype),
        in_specs=[hbm] * 7,
        out_specs=vmem,
        scratch_shapes=[
            pltpu.VMEM(trial.shape, trial.dtype),
            pltpu.SMEM(block_rows.shape, jnp.int32),
            pltpu.SMEM(ent_source.shape, jnp.int32),
            pltpu.SMEM(ent_target.shape, jnp.int32),
            pltpu.SMEM((1, 1), jnp.int32),
            pltpu.VMEM((2, 2, ny, nz, 16, columns // 2), BF16),
            pltpu.VMEM((4 * block_len, columns), BF16),
            pltpu.VMEM((entries, block_len, block_len), BF16),
            pltpu.VMEM((2, block_len, 4 * block_len), BF16),
            pltpu.VMEM((block_len, 4 * block_len), BF16),
            pltpu.VMEM((columns, columns), BF16),
            pltpu.VMEM((columns, columns), BF16),
            pltpu.VMEM((block_len, 2 * columns), BF16),
            pltpu.VMEM((2, chips, 16, columns // 4), BF16),
            pltpu.VMEM((2, 5 * nz, 16, columns // 4), BF16),
            pltpu.VMEM((2, 2, nz, 16, columns // 4), BF16),
            pltpu.VMEM((2, 2, nz // 2, 16, columns // 4), BF16),
            pltpu.VMEM((2, block_len, columns), F32),
            dma((7,)), dma((2,)), dma((2,)), dma((nz,)), dma((nz,)),
            dma((2, far)), dma((2, far)),
            dma((2 * far + 1, nz - 1)), dma((2 * far + 1, nz - 1)),
            dma((2, far, nz)), dma((2, far, nz)),
            dma((2, 2 * far + 1 + nz)), dma((2, 2 * far + 1 + nz)),
            dma((2, 2, 2)), dma((2, 2, 2)),
            dma((2, 5 * nz)), dma((2, 5 * nz)),
        ],
        compiler_params=pltpu.CompilerParams(
            collective_id=0, has_side_effects=True, vmem_limit_bytes=56 * 1024 * 1024,
        ),
        name="sigma",
    )(trial, block_rows, right_ops, left_ops, ent_source, ent_target, ent_count.reshape(1, 1))


def solution(mesh):
    nz = 4
    sectors = mesh.shape["sector"]
    ny = mesh.shape["term"] // (2 * nz)
    placed = (
        P(("sector", "term"), None),
        P("sector"),
        P(("sector", "term"), None, None),
        P(("sector", "term"), None, None, None),
        P(("sector", "term"), None),
        P(("sector", "term"), None),
        P(("sector", "term")),
    )
    return jax.shard_map(
        functools.partial(local, sectors, ny, nz), mesh=mesh, in_specs=placed,
        out_specs=P(("sector", "term"), None), check_vma=False,
    )
```

```python
import functools

import jax
import jax.numpy as jnp
from jax import lax
from jax.experimental import pallas as pl
from jax.experimental.pallas import tpu as pltpu
from jax.sharding import PartitionSpec as P

MESH = pl.DeviceIdType.MESH
F32 = jnp.float32
BF16 = jnp.bfloat16


def kernel(
    sectors, ny, nz,
    trial_in, rows_in, right_ref, left_ref, source_in, target_in, count_in,
    out_ref,
    trial_ref, rows_ref, source_ref, target_ref, count_ref,
    units, window, lefts, weights, stacked, right_own, right_sib, projected, outgoing, incoming,
    passed, passed_half, early,
    load_sem, pair_send, pair_recv, next_send, next_recv, o_send, o_recv, z_send, z_recv, y_send, y_recv,
    d_send, d_recv, m_send, m_recv, r_send, r_recv,
):
    entries, block_len = lefts.shape[0], lefts.shape[1]
    columns = right_own.shape[0]
    half = columns // 2
    group_rows = 2 * block_len
    chips = ny * nz
    far = ny // 2
    s = lax.axis_index("sector")
    t = lax.axis_index("term")
    y, z, c = t // (2 * nz), lax.rem(t // 2, nz), lax.rem(t, 2)
    me = t // 2

    def device(sector, chip, core):
        return (sector, chip * 2 + core)

    sibling = device(s, me, 1 - c)
    following = lax.rem(s + 1, sectors)
    preceding = lax.rem(s + sectors - 1, sectors)

    def near(dy, dz):
        return lax.rem(y + dy + ny, ny) * nz + lax.rem(z + dz, nz)


    loads = [
        pltpu.make_async_copy(source, destination, load_sem.at[i])
        for i, (source, destination) in enumerate([
            (trial_in, trial_ref), (rows_in, rows_ref), (source_in, source_ref), (target_in, target_ref),
            (count_in, count_ref), (left_ref.at[0], lefts), (right_ref.at[0], right_own),
        ])
    ]
    for load in loads:
        load.start()

    barrier = pltpu.get_barrier_semaphore()

    def greet(target):
        pl.semaphore_signal(barrier, inc=1, device_id=target, device_id_type=MESH)

    greet(sibling)

    @pl.when(s > 0)
    def _():
        for dz in range(nz):
            greet(device(preceding, near(0, dz), c))

    for dy in range(-2, 3):
        for dz in range(nz):
            if (dy == 0) != (dz == 0):
                greet(device(s, near(dy, dz), c))

    loads[0].wait()
    loads[1].wait()
    start_row = t * 8
    limit = rows_ref[start_row // block_len]
    inside = lax.rem(start_row, block_len) + lax.broadcasted_iota(jnp.int32, (8, columns), 0)
    live_rows = inside < limit
    rows = jnp.where(live_rows, trial_ref[...].astype(F32), 0.0)
    units[0, c, y, z] = jnp.concatenate([rows[:, :half], rows[:, half:]], axis=0).astype(BF16)

    @pl.when(s < sectors - 1)
    def _():
        pl.semaphore_wait(barrier, 2 * nz + 4)

    @pl.when(s == sectors - 1)
    def _():
        pl.semaphore_wait(barrier, nz + 4)


    def remote(source, destination, send, recv, target):
        return pltpu.make_async_remote_copy(
            src_ref=source, dst_ref=destination, send_sem=send, recv_sem=recv,
            device_id=target, device_id_type=MESH,
        )

    sends = []

    def begin(copy):
        copy.start()
        sends.append(copy)
        return copy

    def behind(way, k):
        return lax.rem(y - k + ny, ny) if way == 0 else lax.rem(y + k, ny)

    def toward(way, hops):
        return device(s, near(hops if way == 0 else -hops, 0), c)

    def own_unit(way, k):
        if k < far:
            return units.at[0, c, behind(way, k), z]
        return units.at[0, c, behind(way, k), z, :, pl.ds(way * (half // 2), half // 2)]

    def index(way, k):
        return way * far + k if k else 0

    def own_step(way, k, hops):
        row = behind(way, k - hops)
        slot = units.at[0, c, row, z] if k < far else units.at[0, c, row, z, :, pl.ds(way * (half // 2), half // 2)]
        return remote(slot, slot, o_send.at[way, k - 1], o_recv.at[way, k - 1], toward(way, hops))

    def own_spread(way, k):
        slot = own_unit(way, k)
        return [
            remote(slot, slot, z_send.at[index(way, k), d - 1], z_recv.at[index(way, k), d - 1], device(s, near(0, d), c))
            for d in range(nz - 1, 0, -1)
        ]

    def prior_unit(way, k, d):
        return units.at[1, c, behind(way, k), lax.rem(z - d + nz, nz)]

    def carried(way, k):
        return range(nz) if k < far else range(way * (nz // 2), (way + 1) * (nz // 2))

    def prior_step(way, k, d, hops):
        slot = prior_unit(way, k - hops, d)
        return remote(slot, slot, y_send.at[way, k - 1, d], y_recv.at[way, k - 1, d], toward(way, hops))

    def pair_copy(st, way, k, d=None):
        slot = units.at[st, c, behind(way, k)] if d is None else prior_unit(way, k, d)
        at = index(way, k) if d is None else 2 * far + 1 + d
        return remote(slot, slot, d_send.at[st, at], d_recv.at[st, at], sibling)

    own, spread = {}, {}
    for way in range(2):
        own[way, 2] = begin(own_step(way, 2, 2))
        own[way, 1] = begin(own_step(way, 1, 1))
    next_all = [
        remote(units.at[0, c, y, z], units.at[1, c, y, z], next_send.at[d], next_recv.at[d],
               device(following, near(0, d), c))
        for d in range(nz)
    ]

    @pl.when(s < sectors - 1)
    def _():
        for copy in next_all:
            copy.start()

    spread[0, 0] = [begin(copy) for copy in own_spread(0, 0)]

    pairs = []

    prior = {
        (way, k, d): prior_step(way, k, d, 2 if k in (2, far) else 1)
        for k in range(1, far + 1) for way in range(2) for d in carried(way, k)
    }
    prior_pairs = {(0, 0): [pair_copy(1, 0, 0)]}
    for k in range(1, far):
        for way in range(2):
            prior_pairs[way, k] = [pair_copy(1, way, k)]
    for way in range(2):
        prior_pairs[way, far] = [pair_copy(1, way, far, d) for d in carried(way, far)]

    def begin_pair(way, k):
        pairs.append(begin(pair_copy(0, way, k)))

    def own_arrival(k):
        for way in range(2):
            own[way, k].wait_recv()
            if k == 2:
                own[way, 3] = begin(own_step(way, 3, 1))
                own[way, far] = begin(own_step(way, far, 2))
            spread[way, k] = [begin(copy) for copy in own_spread(way, k)]

    def own_row(k):
        for way in range(2 if k else 1):
            for copy in spread[way, k]:
                copy.wait_recv()
            if k < far:
                begin_pair(way, k)
        if k == far:
            begin_pair(0, k)

    def prior_arrival(k):
        @pl.when(s > 0)
        def _():
            for d in range(nz):
                if k == 0:
                    next_all[d].wait_recv()
                for way in range(2):
                    if k == 0:
                        prior[way, 2, d].start()
                        prior[way, 1, d].start()
                    elif d in carried(way, k):
                        prior[way, k, d].wait_recv()
                        if k == 2:
                            if d in carried(way, far):
                                prior[way, far, d].start()
                            prior[way, 3, d].start()
                        if k == far:
                            prior_pairs[way, far][d - carried(way, far)[0]].start()
            if k < far:
                for way in range(2 if k else 1):
                    prior_pairs[way, k][0].start()

    own_arrival(1)
    own_arrival(2)
    prior_arrival(0)

    for load in loads[2:6]:
        load.wait()
    count = count_ref[0, 0]
    factors = []
    for k in range(entries):
        live = k < count
        src, dst = source_ref[0, k], target_ref[0, k]
        for b in range(2):
            for w in range(4):
                on = live & (dst == b) & (src == w)
                if w >= 2:
                    on = on & (s > 0)
                factors.append(jnp.where(on, 1.0, 0.0).astype(F32))

    def weigh(i, carry):
        row = pl.multiple_of(i * 32, 32)
        blocks = [lefts[k, pl.ds(row, 32), :].astype(F32) for k in range(entries)]
        at = pl.multiple_of(i * 16, 16)
        for b in range(2):
            for w in range(4):
                total = blocks[0] * factors[b * 4 + w]
                for k in range(1, entries):
                    total = total + blocks[k] * factors[k * 8 + b * 4 + w]
                total = total.reshape(2, 2, 8, block_len)
                for p in range(2):
                    piece = total[:, p].reshape(16, block_len).astype(BF16)
                    weights[p, pl.ds(b * (block_len // 2) + at, 16), w * block_len:(w + 1) * block_len] = piece
        return carry

    lax.fori_loop(0, block_len // 32, weigh, 0)

    right_copy = begin(remote(right_ref.at[0], right_sib, pair_send.at[1], pair_recv.at[1], sibling))
    weights_copy = begin(remote(weights.at[1 - c], stacked.at[pl.ds(block_len, block_len)],
                                pair_send.at[0], pair_recv.at[0], sibling))
    keep = pltpu.make_async_copy(weights.at[c], stacked.at[pl.ds(0, block_len)], load_sem.at[7])
    keep.start()

    own_arrival(3)
    own_arrival(4)
    own_row(0)
    prior_arrival(1)
    own_row(1)
    prior_arrival(2)
    own_row(2)
    own_row(3)
    own_row(4)
    prior_arrival(3)
    prior_arrival(4)

    def lay(st):
        def one(row, carry):
            pieces = [units[st, p, row].astype(F32).reshape(nz, 2, 8, half) for p in range(2)]
            at = pl.multiple_of(st * group_rows + row * (nz * 16), 16)
            for h in range(2):
                both = jnp.concatenate([pieces[0][:, h:h + 1], pieces[1][:, h:h + 1]], axis=1)
                window[pl.ds(at, nz * 16), h * half:(h + 1) * half] = both.reshape(nz * 16, half).astype(BF16)
            return carry

        lax.fori_loop(0, ny, one, 0)

    tile = min(256, half)

    def left_product(st, n):
        rows = slice(st * group_rows, (st + 1) * group_rows)
        return jnp.dot(stacked[:, rows], window[rows, n * tile:(n + 1) * tile], preferred_element_type=F32)

    for copy in pairs:
        copy.wait_recv()
    lay(0)
    weights_copy.wait_recv()
    keep.wait()
    for n in range(columns // tile):
        early[:, n * tile:(n + 1) * tile] = left_product(0, n)

    @pl.when(s > 0)
    def _():
        for copies in prior_pairs.values():
            for copy in copies:
                copy.wait_recv()
        lay(1)

    @pl.when(s == 0)
    def _():
        window[group_rows:, :] = jnp.zeros((group_rows, columns), BF16)

    for n in range(columns // tile):
        at = slice(n * tile, (n + 1) * tile)
        value = (early[:, at] + left_product(1, n)).astype(BF16)
        projected[:, at] = value[:block_len]
        projected[:, columns + n * tile:columns + (n + 1) * tile] = value[block_len:]
    right_copy.wait_recv()
    loads[6].wait()

    def row_at(dy):
        return lax.rem(y + dy + ny, ny) * nz

    part = half // 2
    merged, finals = {}, []

    def deliver(n, dy, dz):
        chip = near(dy, dz)
        at = (2 + dy) * nz
        finals.append(begin(remote(
            outgoing.at[n, chip], incoming.at[n, at + z],
            r_send.at[n, at + dz], r_recv.at[n, at + dz], device(s, chip, c))))

    for n in range(2):
        both = []
        for h in range(2):
            at = h * half + n * part
            value = jnp.dot(projected[:, :columns], right_own[:, at:at + part], preferred_element_type=F32)
            value = value + jnp.dot(projected[:, columns:], right_sib[:, at:at + part], preferred_element_type=F32)
            both.append(value.reshape(chips, 8, part))
        outgoing[n] = jnp.concatenate(both, axis=1).astype(BF16)
        for way, sign in ((0, 1), (1, -1)):
            merged[n, way] = (
                begin(remote(outgoing.at[n, pl.ds(row_at(4) + way * (nz // 2), nz // 2)], passed_half.at[n, way],
                             m_send.at[n, way, 1], m_recv.at[n, way, 1], device(s, near(2 * sign, 0), c))),
                begin(remote(outgoing.at[n, pl.ds(row_at(3 * sign), nz)], passed.at[n, way],
                             m_send.at[n, way, 0], m_recv.at[n, way, 0], device(s, near(sign, 0), c))),
            )

    for n in range(2):
        for dy in (1, -1, 0):
            for dz in range(nz - 1, -1, -1):
                if dy or dz:
                    deliver(n, dy, dz)
        incoming[n, 2 * nz + z] = outgoing[n, me]
    for n in range(2):
        for way, sign in ((0, 1), (1, -1)):
            for copy in merged[n, way]:
                copy.wait_recv()
            for i in range(nz):
                at = row_at(2 * sign) + i
                value = outgoing[n, at].astype(F32) + passed[n, way, i].astype(F32)
                if i // (nz // 2) == way:
                    value = value + passed_half[n, way, i % (nz // 2)].astype(F32)
                outgoing[n, at] = value.astype(BF16)
            for dz in range(nz - 1, -1, -1):
                deliver(n, 2 * sign, dz)

    early_sends = len(sends) - 4 * nz
    for copy in sends[:early_sends]:
        copy.wait_send()

    @pl.when(s > 0)
    def _():
        for copy in prior.values():
            copy.wait_send()
        for copies in prior_pairs.values():
            for copy in copies:
                copy.wait_send()

    @pl.when(s < sectors - 1)
    def _():
        for copy in next_all:
            copy.wait_send()

    for copy in finals:
        copy.wait_recv()
    for n in range(2):
        total = incoming[n, 0].astype(F32)
        for i in range(1, 5 * nz):
            total = total + incoming[n, i].astype(F32)
        for h in range(2):
            at = h * half + n * part
            out_ref[:, at:at + part] = jnp.where(
                live_rows[:, :part], total[h * 8:(h + 1) * 8], 0.0).astype(BF16)

    for copy in sends[early_sends:]:
        copy.wait_send()


def local(sectors, ny, nz, trial, block_rows, right_ops, left_ops, ent_source, ent_target, ent_count):
    entries, block_len = left_ops.shape[1:3]
    columns = trial.shape[1]
    chips = ny * nz
    far = ny // 2
    dma = pltpu.SemaphoreType.DMA
    vmem = pl.BlockSpec(memory_space=pltpu.VMEM)
    hbm = pl.BlockSpec(memory_space=pl.ANY)
    return pl.pallas_call(
        functools.partial(kernel, sectors, ny, nz),
        out_shape=pltpu.VMEM(trial.shape, trial.dtype),
        in_specs=[hbm] * 7,
        out_specs=vmem,
        scratch_shapes=[
            pltpu.VMEM(trial.shape, trial.dtype),
            pltpu.SMEM(block_rows.shape, jnp.int32),
            pltpu.SMEM(ent_source.shape, jnp.int32),
            pltpu.SMEM(ent_target.shape, jnp.int32),
            pltpu.SMEM((1, 1), jnp.int32),
            pltpu.VMEM((2, 2, ny, nz, 16, columns // 2), BF16),
            pltpu.VMEM((4 * block_len, columns), BF16),
            pltpu.VMEM((entries, block_len, block_len), BF16),
            pltpu.VMEM((2, block_len, 4 * block_len), BF16),
            pltpu.VMEM((2 * block_len, 4 * block_len), BF16),
            pltpu.VMEM((columns, columns), BF16),
            pltpu.VMEM((columns, columns), BF16),
            pltpu.VMEM((block_len, 2 * columns), BF16),
            pltpu.VMEM((2, chips, 16, columns // 4), BF16),
            pltpu.VMEM((2, 5 * nz, 16, columns // 4), BF16),
            pltpu.VMEM((2, 2, nz, 16, columns // 4), BF16),
            pltpu.VMEM((2, 2, nz // 2, 16, columns // 4), BF16),
            pltpu.VMEM((2 * block_len, columns), F32),
            dma((8,)), dma((2,)), dma((2,)), dma((nz,)), dma((nz,)),
            dma((2, far)), dma((2, far)),
            dma((2 * far + 1, nz - 1)), dma((2 * far + 1, nz - 1)),
            dma((2, far, nz)), dma((2, far, nz)),
            dma((2, 2 * far + 1 + nz)), dma((2, 2 * far + 1 + nz)),
            dma((2, 2, 2)), dma((2, 2, 2)),
            dma((2, 5 * nz)), dma((2, 5 * nz)),
        ],
        compiler_params=pltpu.CompilerParams(
            collective_id=0, has_side_effects=True, vmem_limit_bytes=56 * 1024 * 1024,
        ),
        name="sigma",
    )(trial, block_rows, right_ops, left_ops, ent_source, ent_target, ent_count.reshape(1, 1))


def solution(mesh):
    nz = 4
    sectors = mesh.shape["sector"]
    ny = mesh.shape["term"] // (2 * nz)
    placed = (
        P(("sector", "term"), None),
        P("sector"),
        P(("sector", "term"), None, None),
        P(("sector", "term"), None, None, None),
        P(("sector", "term"), None),
        P(("sector", "term"), None),
        P(("sector", "term")),
    )
    return jax.shard_map(
        functools.partial(local, sectors, ny, nz), mesh=mesh, in_specs=placed,
        out_specs=P(("sector", "term"), None), check_vma=False,
    )
```

```python
import functools

import jax
import jax.numpy as jnp
from jax import lax
from jax.experimental import pallas as pl
from jax.experimental.pallas import tpu as pltpu
from jax.sharding import PartitionSpec as P

MESH = pl.DeviceIdType.MESH
F32 = jnp.float32
BF16 = jnp.bfloat16


def kernel(
    sectors, ny, nz,
    trial_in, rows_in, right_ref, left_ref, source_in, target_in, count_in,
    out_ref,
    trial_ref, rows_ref, source_ref, target_ref, count_ref,
    units, window, lefts, weights, stacked, right_own, right_sib, projected, outgoing, incoming,
    passed, passed_half, early,
    load_sem, pair_send, pair_recv, next_send, next_recv, o_send, o_recv, z_send, z_recv, y_send, y_recv,
    d_send, d_recv, m_send, m_recv, r_send, r_recv,
):
    entries, block_len = lefts.shape[0], lefts.shape[1]
    columns = right_own.shape[0]
    half = columns // 2
    group_rows = 2 * block_len
    chips = ny * nz
    far = ny // 2
    s = lax.axis_index("sector")
    t = lax.axis_index("term")
    y, z, c = t // (2 * nz), lax.rem(t // 2, nz), lax.rem(t, 2)
    me = t // 2

    def device(sector, chip, core):
        return (sector, chip * 2 + core)

    sibling = device(s, me, 1 - c)
    following = lax.rem(s + 1, sectors)
    preceding = lax.rem(s + sectors - 1, sectors)

    def near(dy, dz):
        return lax.rem(y + dy + ny, ny) * nz + lax.rem(z + dz, nz)


    loads = [
        pltpu.make_async_copy(source, destination, load_sem.at[i])
        for i, (source, destination) in enumerate([
            (trial_in, trial_ref), (rows_in, rows_ref), (source_in, source_ref), (target_in, target_ref),
            (count_in, count_ref), (left_ref.at[0], lefts), (right_ref.at[0], right_own),
        ])
    ]
    for load in loads:
        load.start()

    barrier = pltpu.get_barrier_semaphore()

    def greet(target):
        pl.semaphore_signal(barrier, inc=1, device_id=target, device_id_type=MESH)

    greet(sibling)

    @pl.when(s > 0)
    def _():
        for dz in range(nz):
            greet(device(preceding, near(0, dz), c))

    for dy in range(-2, 3):
        for dz in range(nz):
            if (dy == 0) != (dz == 0):
                greet(device(s, near(dy, dz), c))

    loads[0].wait()
    loads[1].wait()
    start_row = t * 8
    limit = rows_ref[start_row // block_len]
    inside = lax.rem(start_row, block_len) + lax.broadcasted_iota(jnp.int32, (8, columns), 0)
    live_rows = inside < limit
    rows = jnp.where(live_rows, trial_ref[...].astype(F32), 0.0)
    units[0, c, y, z] = jnp.concatenate([rows[:, :half], rows[:, half:]], axis=0).astype(BF16)

    @pl.when(s < sectors - 1)
    def _():
        pl.semaphore_wait(barrier, 2 * nz + 4)

    @pl.when(s == sectors - 1)
    def _():
        pl.semaphore_wait(barrier, nz + 4)


    def remote(source, destination, send, recv, target):
        return pltpu.make_async_remote_copy(
            src_ref=source, dst_ref=destination, send_sem=send, recv_sem=recv,
            device_id=target, device_id_type=MESH,
        )

    sends = []

    def begin(copy):
        copy.start()
        sends.append(copy)
        return copy

    def behind(way, k):
        return lax.rem(y - k + ny, ny) if way == 0 else lax.rem(y + k, ny)

    def toward(way, hops):
        return device(s, near(hops if way == 0 else -hops, 0), c)

    def own_unit(way, k):
        if k < far:
            return units.at[0, c, behind(way, k), z]
        return units.at[0, c, behind(way, k), z, :, pl.ds(way * (half // 2), half // 2)]

    def index(way, k):
        return way * far + k if k else 0

    def own_step(way, k, hops):
        row = behind(way, k - hops)
        slot = units.at[0, c, row, z] if k < far else units.at[0, c, row, z, :, pl.ds(way * (half // 2), half // 2)]
        return remote(slot, slot, o_send.at[way, k - 1], o_recv.at[way, k - 1], toward(way, hops))

    def own_spread(way, k):
        slot = own_unit(way, k)
        return [
            remote(slot, slot, z_send.at[index(way, k), d - 1], z_recv.at[index(way, k), d - 1], device(s, near(0, d), c))
            for d in range(nz - 1, 0, -1)
        ]

    def prior_unit(way, k, d):
        return units.at[1, c, behind(way, k), lax.rem(z - d + nz, nz)]

    def carried(way, k):
        return range(nz) if k < far else range(way * (nz // 2), (way + 1) * (nz // 2))

    def prior_step(way, k, d, hops):
        slot = prior_unit(way, k - hops, d)
        return remote(slot, slot, y_send.at[way, k - 1, d], y_recv.at[way, k - 1, d], toward(way, hops))

    def pair_copy(st, way, k, d=None):
        slot = units.at[st, c, behind(way, k)] if d is None else prior_unit(way, k, d)
        at = index(way, k) if d is None else 2 * far + 1 + d
        return remote(slot, slot, d_send.at[st, at], d_recv.at[st, at], sibling)

    own, spread = {}, {}
    for way in range(2):
        own[way, 2] = begin(own_step(way, 2, 2))
        own[way, 1] = begin(own_step(way, 1, 1))
    next_all = [
        remote(units.at[0, c, y, z], units.at[1, c, y, z], next_send.at[d], next_recv.at[d],
               device(following, near(0, d), c))
        for d in range(nz)
    ]

    @pl.when(s < sectors - 1)
    def _():
        for copy in next_all:
            copy.start()

    spread[0, 0] = [begin(copy) for copy in own_spread(0, 0)]

    pairs = []

    prior = {
        (way, k, d): prior_step(way, k, d, 2 if k in (2, far) else 1)
        for k in range(1, far + 1) for way in range(2) for d in carried(way, k)
    }
    prior_pairs = {(0, 0): [pair_copy(1, 0, 0)]}
    for k in range(1, far):
        for way in range(2):
            prior_pairs[way, k] = [pair_copy(1, way, k)]
    for way in range(2):
        prior_pairs[way, far] = [pair_copy(1, way, far, d) for d in carried(way, far)]

    def begin_pair(way, k):
        pairs.append(begin(pair_copy(0, way, k)))

    def own_arrival(k):
        for way in range(2):
            own[way, k].wait_recv()
            if k == 2:
                own[way, 3] = begin(own_step(way, 3, 1))
                own[way, far] = begin(own_step(way, far, 2))
            spread[way, k] = [begin(copy) for copy in own_spread(way, k)]

    def own_row(k):
        for way in range(2 if k else 1):
            for copy in spread[way, k]:
                copy.wait_recv()
            if k < far:
                begin_pair(way, k)
        if k == far:
            begin_pair(0, k)

    def prior_arrival(k):
        @pl.when(s > 0)
        def _():
            for d in range(nz):
                if k == 0:
                    next_all[d].wait_recv()
                for way in range(2):
                    if k == 0:
                        prior[way, 2, d].start()
                        prior[way, 1, d].start()
                    elif d in carried(way, k):
                        prior[way, k, d].wait_recv()
                        if k == 2:
                            if d in carried(way, far):
                                prior[way, far, d].start()
                            prior[way, 3, d].start()
                        if k == far:
                            prior_pairs[way, far][d - carried(way, far)[0]].start()
            if k < far:
                for way in range(2 if k else 1):
                    prior_pairs[way, k][0].start()

    own_arrival(1)
    own_arrival(2)
    prior_arrival(0)

    for load in loads[2:6]:
        load.wait()
    count = count_ref[0, 0]
    factors = []
    for k in range(entries):
        live = k < count
        src, dst = source_ref[0, k], target_ref[0, k]
        for b in range(2):
            for w in range(4):
                on = live & (dst == b) & (src == w)
                if w >= 2:
                    on = on & (s > 0)
                factors.append(jnp.where(on, 1.0, 0.0).astype(F32))

    def weigh(i, carry):
        row = pl.multiple_of(i * 32, 32)
        blocks = [lefts[k, pl.ds(row, 32), :].astype(F32) for k in range(entries)]
        at = pl.multiple_of(i * 16, 16)
        for b in range(2):
            for w in range(4):
                total = blocks[0] * factors[b * 4 + w]
                for k in range(1, entries):
                    total = total + blocks[k] * factors[k * 8 + b * 4 + w]
                total = total.reshape(2, 2, 8, block_len)
                for p in range(2):
                    piece = total[:, p].reshape(16, block_len).astype(BF16)
                    weights[p, pl.ds(b * (block_len // 2) + at, 16), w * block_len:(w + 1) * block_len] = piece
        return carry

    lax.fori_loop(0, block_len // 32, weigh, 0)

    right_copy = begin(remote(right_ref.at[0], right_sib, pair_send.at[1], pair_recv.at[1], sibling))
    weights_copy = begin(remote(weights.at[1 - c], stacked.at[pl.ds(block_len, block_len)],
                                pair_send.at[0], pair_recv.at[0], sibling))
    keep = pltpu.make_async_copy(weights.at[c], stacked.at[pl.ds(0, block_len)], load_sem.at[7])
    keep.start()

    own_arrival(3)
    own_arrival(4)
    own_row(0)
    prior_arrival(1)
    own_row(1)
    prior_arrival(2)
    own_row(2)
    own_row(3)
    own_row(4)
    prior_arrival(3)
    prior_arrival(4)

    def lay(st):
        def one(row, carry):
            pieces = [units[st, p, row].astype(F32).reshape(nz, 2, 8, half) for p in range(2)]
            at = pl.multiple_of(st * group_rows + row * (nz * 16), 16)
            for h in range(2):
                both = jnp.concatenate([pieces[0][:, h:h + 1], pieces[1][:, h:h + 1]], axis=1)
                window[pl.ds(at, nz * 16), h * half:(h + 1) * half] = both.reshape(nz * 16, half).astype(BF16)
            return carry

        lax.fori_loop(0, ny, one, 0)

    tile = half

    def left_product(st, n):
        rows = slice(st * group_rows, (st + 1) * group_rows)
        return jnp.dot(stacked[:, rows], window[rows, n * tile:(n + 1) * tile], preferred_element_type=F32)

    for copy in pairs:
        copy.wait_recv()
    lay(0)
    weights_copy.wait_recv()
    keep.wait()
    for n in range(columns // tile):
        early[:, n * tile:(n + 1) * tile] = left_product(0, n)

    @pl.when(s > 0)
    def _():
        for copies in prior_pairs.values():
            for copy in copies:
                copy.wait_recv()
        lay(1)

    @pl.when(s == 0)
    def _():
        window[group_rows:, :] = jnp.zeros((group_rows, columns), BF16)

    for n in range(columns // tile):
        at = slice(n * tile, (n + 1) * tile)
        value = (early[:, at] + left_product(1, n)).astype(BF16)
        projected[:, at] = value[:block_len]
        projected[:, columns + n * tile:columns + (n + 1) * tile] = value[block_len:]
    right_copy.wait_recv()
    loads[6].wait()

    def row_at(dy):
        return lax.rem(y + dy + ny, ny) * nz

    part = half // 2
    merged, finals = {}, []

    def deliver(n, dy, dz):
        chip = near(dy, dz)
        at = (2 + dy) * nz
        finals.append(begin(remote(
            outgoing.at[n, chip], incoming.at[n, at + z],
            r_send.at[n, at + dz], r_recv.at[n, at + dz], device(s, chip, c))))

    for n in range(2):
        both = []
        for h in range(2):
            at = h * half + n * part
            value = jnp.dot(projected[:, :columns], right_own[:, at:at + part], preferred_element_type=F32)
            value = value + jnp.dot(projected[:, columns:], right_sib[:, at:at + part], preferred_element_type=F32)
            both.append(value.reshape(chips, 8, part))
        outgoing[n] = jnp.concatenate(both, axis=1).astype(BF16)
        for way, sign in ((0, 1), (1, -1)):
            merged[n, way] = (
                begin(remote(outgoing.at[n, pl.ds(row_at(4) + way * (nz // 2), nz // 2)], passed_half.at[n, way],
                             m_send.at[n, way, 1], m_recv.at[n, way, 1], device(s, near(2 * sign, 0), c))),
                begin(remote(outgoing.at[n, pl.ds(row_at(3 * sign), nz)], passed.at[n, way],
                             m_send.at[n, way, 0], m_recv.at[n, way, 0], device(s, near(sign, 0), c))),
            )

    for n in range(2):
        for dy in (1, -1, 0):
            for dz in range(nz - 1, -1, -1):
                if dy or dz:
                    deliver(n, dy, dz)
        incoming[n, 2 * nz + z] = outgoing[n, me]
    for n in range(2):
        for way, sign in ((0, 1), (1, -1)):
            for copy in merged[n, way]:
                copy.wait_recv()
            for i in range(nz):
                at = row_at(2 * sign) + i
                value = outgoing[n, at].astype(F32) + passed[n, way, i].astype(F32)
                if i // (nz // 2) == way:
                    value = value + passed_half[n, way, i % (nz // 2)].astype(F32)
                outgoing[n, at] = value.astype(BF16)
            for dz in range(nz - 1, -1, -1):
                deliver(n, 2 * sign, dz)

    early_sends = len(sends) - 4 * nz
    for copy in sends[:early_sends]:
        copy.wait_send()

    @pl.when(s > 0)
    def _():
        for copy in prior.values():
            copy.wait_send()
        for copies in prior_pairs.values():
            for copy in copies:
                copy.wait_send()

    @pl.when(s < sectors - 1)
    def _():
        for copy in next_all:
            copy.wait_send()

    for copy in finals:
        copy.wait_recv()
    for n in range(2):
        total = incoming[n, 0].astype(F32)
        for i in range(1, 5 * nz):
            total = total + incoming[n, i].astype(F32)
        for h in range(2):
            at = h * half + n * part
            out_ref[:, at:at + part] = jnp.where(
                live_rows[:, :part], total[h * 8:(h + 1) * 8], 0.0).astype(BF16)

    for copy in sends[early_sends:]:
        copy.wait_send()


def local(sectors, ny, nz, trial, block_rows, right_ops, left_ops, ent_source, ent_target, ent_count):
    entries, block_len = left_ops.shape[1:3]
    columns = trial.shape[1]
    chips = ny * nz
    far = ny // 2
    dma = pltpu.SemaphoreType.DMA
    vmem = pl.BlockSpec(memory_space=pltpu.VMEM)
    hbm = pl.BlockSpec(memory_space=pl.ANY)
    return pl.pallas_call(
        functools.partial(kernel, sectors, ny, nz),
        out_shape=pltpu.VMEM(trial.shape, trial.dtype),
        in_specs=[hbm] * 7,
        out_specs=vmem,
        scratch_shapes=[
            pltpu.VMEM(trial.shape, trial.dtype),
            pltpu.SMEM(block_rows.shape, jnp.int32),
            pltpu.SMEM(ent_source.shape, jnp.int32),
            pltpu.SMEM(ent_target.shape, jnp.int32),
            pltpu.SMEM((1, 1), jnp.int32),
            pltpu.VMEM((2, 2, ny, nz, 16, columns // 2), BF16),
            pltpu.VMEM((4 * block_len, columns), BF16),
            pltpu.VMEM((entries, block_len, block_len), BF16),
            pltpu.VMEM((2, block_len, 4 * block_len), BF16),
            pltpu.VMEM((2 * block_len, 4 * block_len), BF16),
            pltpu.VMEM((columns, columns), BF16),
            pltpu.VMEM((columns, columns), BF16),
            pltpu.VMEM((block_len, 2 * columns), BF16),
            pltpu.VMEM((2, chips, 16, columns // 4), BF16),
            pltpu.VMEM((2, 5 * nz, 16, columns // 4), BF16),
            pltpu.VMEM((2, 2, nz, 16, columns // 4), BF16),
            pltpu.VMEM((2, 2, nz // 2, 16, columns // 4), BF16),
            pltpu.VMEM((2 * block_len, columns), F32),
            dma((8,)), dma((2,)), dma((2,)), dma((nz,)), dma((nz,)),
            dma((2, far)), dma((2, far)),
            dma((2 * far + 1, nz - 1)), dma((2 * far + 1, nz - 1)),
            dma((2, far, nz)), dma((2, far, nz)),
            dma((2, 2 * far + 1 + nz)), dma((2, 2 * far + 1 + nz)),
            dma((2, 2, 2)), dma((2, 2, 2)),
            dma((2, 5 * nz)), dma((2, 5 * nz)),
        ],
        compiler_params=pltpu.CompilerParams(
            collective_id=0, has_side_effects=True, vmem_limit_bytes=56 * 1024 * 1024,
        ),
        name="sigma",
    )(trial, block_rows, right_ops, left_ops, ent_source, ent_target, ent_count.reshape(1, 1))


def solution(mesh):
    nz = 4
    sectors = mesh.shape["sector"]
    ny = mesh.shape["term"] // (2 * nz)
    placed = (
        P(("sector", "term"), None),
        P("sector"),
        P(("sector", "term"), None, None),
        P(("sector", "term"), None, None, None),
        P(("sector", "term"), None),
        P(("sector", "term"), None),
        P(("sector", "term")),
    )
    return jax.shard_map(
        functools.partial(local, sectors, ny, nz), mesh=mesh, in_specs=placed,
        out_specs=P(("sector", "term"), None), check_vma=False,
    )
```
